128 devices in a mesh: orb: 4 (over y_lo, core), grid: 32 (over x, y_hi, z).
Axes of the slice: x: 4, y: 4 (y_hi: 2, y_lo: 2; y = y_hi * 2 + y_lo), z: 4, core: 2. Of those that a mesh axis runs over, the one named last changes fastest.
Arguments:
- orbitals: bfloat16 [8192, 49152], P('orb', 'grid'), may hold values from -7 to 7, as said below
- block_order: int32 [16], replicated, may hold values from 0 to 15, each once
Outputs:
- factor_rows: float32 [1024, 8192], P(None, 'orb')
- ortho: float32 [1024, 49152], P('orb', 'grid')
The draws below stay inside these ranges and needn't reach their ends.
Inputs may be any that keep to these rules, and one draw needn't show every extreme that they name: `block_order`: each block number appears once. `orbitals`: orbitals are linearly independent and of order one.
All inputs are finite; a program needn't handle non-finite values.
Results may differ from the reference program's by a relative error of at most 0.0003.
Values may be sent and summed in bfloat16 or wider, within the bound.
A program may use at most 128 MiB of HBM per device.

```python
import jax
import jax.numpy as jnp
from jax import lax

B = 512
NB = 16
NORB = 8192
NCELL = 49152


def draw_orbitals(key, part):
    key = jax.random.fold_in(key, 11)
    base_draw = jnp.clip(jax.random.normal(key, (NORB, NCELL), jnp.float32), -5.0, 5.0)
    mixed_rows = base_draw
    for shift_rows in (3 * B + 1, 5 * B + 3, 9 * B + 5, 13 * B + 7):
        mixed_rows = mixed_rows + 0.1 * jnp.roll(base_draw, shift_rows, axis=0)
    return mixed_rows.astype(jnp.bfloat16)


def setup_inputs(seed: int = 0) -> dict:
    arg_keys = jax.random.split(jax.random.key(seed), 3)
    orbitals = draw_orbitals(jax.random.fold_in(arg_keys[2], 71), 0)
    block_order = jax.random.permutation(arg_keys[1], NB).astype(jnp.int32)
    return {"orbitals": orbitals, "block_order": block_order}


def factor_pieces(diag_tiles):
    identity = jnp.eye(B, dtype=jnp.float32)
    first_chol = jnp.linalg.cholesky(diag_tiles[:B, :B])
    first_inv = jax.scipy.linalg.solve_triangular(first_chol, identity, lower=True)
    coupling = jnp.dot(first_inv, diag_tiles[:B, B:], precision=lax.Precision.HIGHEST)
    schur_block = diag_tiles[B:, B:] - jnp.dot(coupling.T, coupling, precision=lax.Precision.HIGHEST)
    second_chol = jnp.linalg.cholesky(schur_block)
    second_inv = jax.scipy.linalg.solve_triangular(second_chol, identity, lower=True)
    lower_part = -jnp.dot(jnp.dot(second_inv, coupling.T, precision=lax.Precision.HIGHEST), first_inv, precision=lax.Precision.HIGHEST)
    empty_tile = jnp.zeros((B, B), jnp.float32)
    mixing = jnp.concatenate([jnp.concatenate([first_inv, empty_tile], 1), jnp.concatenate([lower_part, second_inv], 1)], 0)
    return (first_inv, coupling, second_inv, mixing)

def triangular_rows(gram_rows, first_inv, coupling, second_inv, column_blocks, first_block):
    upper_first = jnp.dot(first_inv, gram_rows[:B], precision=lax.Precision.HIGHEST)
    reduced = gram_rows[B:] - jnp.dot(coupling.T, upper_first, precision=lax.Precision.HIGHEST)
    upper_second = jnp.dot(second_inv, reduced, precision=lax.Precision.HIGHEST)
    upper_second = jnp.where((column_blocks == first_block)[None, :], jnp.float32(0.0), upper_second)
    return jnp.concatenate([upper_first, upper_second], 0)

def reference(orbitals, block_order):
    first_block = block_order[0].astype(jnp.int32)
    second_block = block_order[1].astype(jnp.int32)
    panel = jnp.concatenate([lax.dynamic_slice_in_dim(orbitals, first_block * B, B, 0), lax.dynamic_slice_in_dim(orbitals, second_block * B, B, 0)], 0)
    summed = lax.dot_general(panel.astype(jnp.float32), orbitals.astype(jnp.float32), (((1,), (1,)), ((), ())), preferred_element_type=jnp.float32)
    gram_rows = summed * (1.0 / NCELL)
    diag_tiles = jnp.concatenate([lax.dynamic_slice_in_dim(gram_rows, first_block * B, B, 1), lax.dynamic_slice_in_dim(gram_rows, second_block * B, B, 1)], 1)
    first_inv, coupling, second_inv, mixing = factor_pieces(diag_tiles)
    column_blocks = jnp.arange(NORB, dtype=jnp.int32) // B
    factor_rows = triangular_rows(gram_rows, first_inv, coupling, second_inv, column_blocks, first_block)
    ortho = jnp.dot(mixing, panel.astype(jnp.float32), precision=lax.Precision.HIGHEST)
    return (factor_rows, ortho)
```

```python
import jax
import jax.numpy as jnp
from jax import lax
from jax.experimental import pallas as pl
from jax.experimental.pallas import tpu as pltpu
from jax.sharding import PartitionSpec as P

B = 512
BPD = 4
BLK = 128
SUB = 8
HI = lax.Precision.HIGHEST


def invert_block(block_ref, out_ref):
    shape = (SUB, BLK)
    lane = lax.broadcasted_iota(jnp.int32, shape, 1)
    row = lax.broadcasted_iota(jnp.int32, shape, 0)
    count = BLK // SUB
    tiles = [block_ref[SUB * i : SUB * i + SUB, :] for i in range(count)]
    for c in range(count):
        low = SUB * c
        here = jnp.logical_and(lane >= low, lane < low + SUB)
        pivot = tiles[c]
        column = [jnp.broadcast_to(pivot[:, low + m : low + m + 1], shape) for m in range(SUB)]
        a = {}
        for m in range(SUB):
            for i in range(m, SUB):
                a[i, m] = jnp.broadcast_to(column[m][i : i + 1, :], shape)
        marked = jnp.where(here, (lane - low == row).astype(jnp.float32), pivot)
        y = [jnp.broadcast_to(marked[k : k + 1, :], shape) for k in range(SUB)]
        t = {}
        for m in range(SUB):
            r = lax.rsqrt(a[m, m])
            for i in range(m + 1, SUB):
                a[i, m] = a[i, m] * r
            y[m] = y[m] * r
            for k in range(m):
                t[m, k] = t[m, k] * r
            t[m, m] = r
            for j in range(m + 1, SUB):
                for i in range(j, SUB):
                    a[i, j] = a[i, j] - a[i, m] * a[j, m]
            for i in range(m + 1, SUB):
                y[i] = y[i] - a[i, m] * y[m]
                for k in range(m):
                    t[i, k] = t[i, k] - a[i, m] * t[m, k]
                t[i, m] = -(a[i, m] * r)
        tile = y[0]
        for i in range(1, SUB):
            tile = jnp.where(row == i, y[i], tile)
        out_ref[low : low + SUB, :] = jnp.where(lane < low + SUB, tile, 0.0)
        if c == count - 1:
            break
        z = []
        for k in range(SUB):
            acc = t[k, k] * y[k]
            for i in range(k + 1, SUB):
                acc = acc + t[i, k] * y[i]
            z.append(acc)
        for r in range(c + 1, count):
            terms = [jnp.broadcast_to(tiles[r][:, low + m : low + m + 1], shape) * z[m] for m in range(SUB)]
            while len(terms) > 1:
                terms = [terms[i] + terms[i + 1] for i in range(0, len(terms), 2)]
            tiles[r] = jnp.where(here, 0.0, tiles[r]) - terms[0]


def inverse_factor_kernel(g_ref, out_ref, work, block, inv):
    n = g_ref.shape[0]
    count = n // BLK
    work[...] = g_ref[...]
    column = lax.broadcasted_iota(jnp.int32, (BLK, n), 1)

    def step(k, carry):
        start = pl.multiple_of(k * BLK, BLK)
        here = pl.ds(start, BLK)
        block[...] = work[here, here]
        invert_block(block, inv)
        t = inv[...]
        row = jnp.dot(t, work[here, :], precision=HI, preferred_element_type=jnp.float32)
        out_ref[here, :] = jnp.where(column < start, row, 0.0)
        out_ref[here, here] = t
        work[here, :] = row
        work[here, here] = t

        def update(i, carry):
            rows = pl.ds(pl.multiple_of(i * BLK, BLK), BLK)
            u = work[here, rows]
            work[rows, here] = jnp.zeros((BLK, BLK), jnp.float32)
            work[rows, :] -= lax.dot_general(
                u, work[here, :], (((0,), (0,)), ((), ())), precision=HI, preferred_element_type=jnp.float32
            )
            return carry

        return lax.fori_loop(k + 1, count, update, carry)

    lax.fori_loop(0, count, step, 0)


def inverse_factor(g):
    n = g.shape[0]
    return pl.pallas_call(
        inverse_factor_kernel,
        out_shape=jax.ShapeDtypeStruct((n, n), jnp.float32),
        in_specs=[pl.BlockSpec(memory_space=pltpu.VMEM)],
        out_specs=pl.BlockSpec(memory_space=pltpu.VMEM),
        scratch_shapes=[
            pltpu.VMEM((n, n), jnp.float32),
            pltpu.VMEM((BLK, BLK), jnp.float32),
            pltpu.VMEM((BLK, BLK), jnp.float32),
        ],
        compiler_params=pltpu.CompilerParams(vmem_limit_bytes=40 << 20),
    )(g)


CELLS = 49152
ROWS = 2 * B
MAIN = 1280
WIDE = 1024
RING = 4
MESH = pl.DeviceIdType.MESH


def gram_kernel(cand_ref, orb_ref, panel_out, gram_out, diag_out,
                panel, merged, from_core, from_chip, gram, first, second, third, diag,
                panel_send, panel_recv, send, recv, free, local):
    o = lax.axis_index("orb")
    g = lax.axis_index("grid")
    core = o % 2
    mate = o + 1 - 2 * core
    across = (o + 2) % 4
    x = g // 8
    y = (g // 4) % 2
    z = g % 4
    x_next = ((x + 1) % RING) * 8 + y * 4 + z
    x_prev = ((x + 3) % RING) * 8 + y * 4 + z
    z_next = x * 8 + y * 4 + (z + 1) % RING
    z_prev = x * 8 + y * 4 + (z + 3) % RING
    y_mate = x * 8 + (1 - y) * 4 + z

    barrier = pltpu.get_barrier_semaphore()
    for other in (mate, across):
        pl.semaphore_signal(barrier, inc=1, device_id={"orb": other}, device_id_type=MESH)
    for other in (x_next, x_prev, z_next, z_prev, y_mate):
        pl.semaphore_signal(barrier, inc=1, device_id={"grid": other}, device_id_type=MESH)
    pl.semaphore_wait(barrier, 7)

    piece = B // PIECES
    mine = core * B
    theirs = (1 - core) * B

    def part(start, j):
        return pl.ds(pl.multiple_of(start + j * piece, piece), piece)

    def orb_copy(src, dst, other, index):
        return pltpu.make_async_remote_copy(
            src_ref=src, dst_ref=dst, send_sem=panel_send.at[index], recv_sem=panel_recv.at[index],
            device_id={"orb": other}, device_id_type=MESH)

    a = [orb_copy(cand_ref.at[part(theirs, j)], from_core.at[j], mate, j) for j in range(PIECES)]
    b = [orb_copy(merged.at[j], from_chip.at[j], across, PIECES + j) for j in range(PIECES)]
    c = [orb_copy(panel.at[part(mine, j)], panel.at[part(mine, j)], mate, 2 * PIECES + j) for j in range(PIECES)]
    for copy in a:
        copy.start()
    for j in range(PIECES):
        a[j].wait_recv()
        merged[j] = cand_ref[part(mine, j), :] + from_core[j]
        b[j].start()
    for j in range(PIECES):
        b[j].wait_recv()
        panel[part(mine, j), :] = merged[j] + from_chip[j]
        c[j].start()
    for j in range(PIECES):
        c[j].wait_recv()
    for copy in a + b + c:
        copy.wait_send()
    save_panel = pltpu.make_async_copy(panel, panel_out, local.at[0])
    save_panel.start()

    contract = (((1,), (1,)), ((), ()))
    tile = 256

    for h in range(2):
        def column(n, carry, h=h):
            at = pl.multiple_of(n * tile, tile)
            gram[h, :ROWS, pl.ds(at, tile)] = lax.dot_general(
                panel[...], orb_ref[pl.ds(h * WIDE + at, tile), :], contract, preferred_element_type=jnp.float32)
            gram[h, ROWS:, pl.ds(at, tile)] = lax.dot_general(
                panel[pl.ds(pl.multiple_of(core * B + h * 256, 256), 256), :], panel[pl.ds(at, tile), :],
                contract, preferred_element_type=jnp.float32)
            return carry

        lax.fori_loop(0, WIDE // tile, column, 0)

    count = [0]
    started = []

    def grid_copy(src, dst, other):
        index = count[0]
        count[0] += 1
        copy = pltpu.make_async_remote_copy(
            src_ref=src, dst_ref=dst, send_sem=send.at[index], recv_sem=recv.at[index],
            device_id={"grid": other}, device_id_type=MESH)
        copy.start()
        started.append(copy)
        return copy

    def sent(*copies):
        for copy in copies:
            copy.wait_send()
            started[:] = [other for other in started if other is not copy]

    def reduce_ring(h, p, following, previous, base, size, slots, spare):
        half = size // 2

        def rows(q, which):
            return pl.ds(pl.multiple_of(base + ((p + q) % RING) * size + which * half, 8), half)

        data = gram.at[h]
        far_f = grid_copy(data.at[rows(2, 0)], slots.at[0], following)
        far_b = grid_copy(data.at[rows(2, 1)], slots.at[1], previous)
        near_f = grid_copy(data.at[rows(1, 1)], slots.at[2], following)
        near_b = grid_copy(data.at[rows(3, 0)], slots.at[3], previous)
        yield
        far_f.wait_recv()
        slots[0] = slots[0] + gram[h, rows(1, 0), :]
        sum_f = grid_copy(slots.at[0], slots.at[4], following)
        far_b.wait_recv()
        slots[1] = slots[1] + gram[h, rows(3, 1), :]
        sum_b = grid_copy(slots.at[1], slots.at[5], previous)
        yield
        near_f.wait_recv()
        near_b.wait_recv()
        sum_f.wait_recv()
        gram[h, rows(0, 0), :] = gram[h, rows(0, 0), :] + (slots[3] + slots[4])
        sum_b.wait_recv()
        gram[h, rows(0, 1), :] = gram[h, rows(0, 1), :] + (slots[2] + slots[5])
        sent(far_f, far_b, near_f, near_b)
        for other in (following, previous):
            pl.semaphore_signal(spare, inc=1, device_id={"grid": other}, device_id_type=MESH)

    def gather_ring(h, p, following, previous, base, size, spare):
        half = size // 2
        data = gram.at[h]

        def rows(q, which):
            return data.at[pl.ds(pl.multiple_of(base + ((p + q) % RING) * size + which * half, 8), half)]

        own = data.at[pl.ds(pl.multiple_of(base + p * size, 8), size)]
        pl.semaphore_wait(spare, 2)
        near_f = grid_copy(own, own, following)
        near_b = grid_copy(own, own, previous)
        yield
        near_f.wait_recv()
        far_f = grid_copy(rows(3, 0), rows(3, 0), following)
        near_b.wait_recv()
        far_b = grid_copy(rows(1, 1), rows(1, 1), previous)
        yield
        far_f.wait_recv()
        far_b.wait_recv()

    def all_reduce(h, p, following, previous, q, q_following, q_previous, slots):
        one = MAIN // RING
        two = one // RING
        three = two // 2
        base = p * one
        low = base + q * two
        yield from reduce_ring(h, p, following, previous, 0, one, slots[0], free.at[h, 0])
        yield from reduce_ring(h, q, q_following, q_previous, base, two, slots[1], free.at[h, 1])
        own = pl.ds(pl.multiple_of(low + y * three, 8), three)
        rest = pl.ds(pl.multiple_of(low + (1 - y) * three, 8), three)
        swap = grid_copy(gram.at[h, rest], slots[2], y_mate)
        yield
        swap.wait_recv()
        gram[h, own, :] = gram[h, own, :] + slots[2][...]
        share = grid_copy(gram.at[h, own], slots[3], y_mate)
        yield
        share.wait_recv()
        sent(swap)
        gram[h, rest, :] = slots[3][...]
        yield from gather_ring(h, q, q_following, q_previous, base, two, free.at[h, 1])
        yield from gather_ring(h, p, following, previous, 0, one, free.at[h, 0])

    runs = [
        all_reduce(0, x, x_next, x_prev, z, z_next, z_prev, [first.at[0], second.at[0], third.at[0], third.at[1]]),
        all_reduce(1, z, z_next, z_prev, x, x_next, x_prev, [first.at[1], second.at[1], third.at[2], third.at[3]]),
    ]
    while runs:
        for run in list(runs):
            try:
                next(run)
            except StopIteration:
                runs.remove(run)

    saves = []
    shares = []
    for h in range(2):
        shares.append(orb_copy(gram.at[h, pl.ds(ROWS, 256)], diag.at[h], mate, 3 * PIECES + h))
        shares[-1].start()
        saves.append(pltpu.make_async_copy(
            gram.at[h, pl.ds(0, ROWS)], gram_out.at[:, pl.ds(h * WIDE, WIDE)], local.at[1 + h]))
        saves.append(pltpu.make_async_copy(
            gram.at[h, pl.ds(ROWS, 256)], diag_out.at[pl.ds(pl.multiple_of(core * B + h * 256, 256), 256)],
            local.at[3 + h]))
    for save in saves:
        save.start()
    for h in range(2):
        shares[h].wait_recv()
        save = pltpu.make_async_copy(
            diag.at[h], diag_out.at[pl.ds(pl.multiple_of((1 - core) * B + h * 256, 256), 256)], local.at[5 + h])
        save.start()
        saves.append(save)
    for copy in started + shares:
        copy.wait_send()
    save_panel.wait()
    for save in saves:
        save.wait()


PIECES = 4


def gram_sums(cand, orbitals):
    cells = orbitals.shape[1]
    f32 = jnp.float32
    any_space = pl.BlockSpec(memory_space=pl.ANY)
    return pl.pallas_call(
        gram_kernel,
        out_shape=(
            jax.ShapeDtypeStruct((ROWS, cells), jnp.bfloat16),
            jax.ShapeDtypeStruct((ROWS, 2 * WIDE), f32),
            jax.ShapeDtypeStruct((ROWS, ROWS), f32),
        ),
        in_specs=[pl.BlockSpec(memory_space=pltpu.VMEM)] * 2,
        out_specs=(any_space,) * 3,
        scratch_shapes=[
            pltpu.VMEM((ROWS, cells), jnp.bfloat16),
            pltpu.VMEM((PIECES, B // PIECES, cells), jnp.bfloat16),
            pltpu.VMEM((PIECES, B // PIECES, cells), jnp.bfloat16),
            pltpu.VMEM((PIECES, B // PIECES, cells), jnp.bfloat16),
            pltpu.VMEM((2, MAIN, WIDE), f32),
            pltpu.VMEM((2, 6, MAIN // 8, WIDE), f32),
            pltpu.VMEM((2, 6, MAIN // 32, WIDE), f32),
            pltpu.VMEM((4, MAIN // 32, WIDE), f32),
            pltpu.VMEM((2, 256, WIDE), f32),
            pltpu.SemaphoreType.DMA((3 * PIECES + 2,)),
            pltpu.SemaphoreType.DMA((3 * PIECES + 2,)),
            pltpu.SemaphoreType.DMA((44,)),
            pltpu.SemaphoreType.DMA((44,)),
            pltpu.SemaphoreType.REGULAR((2, 2)),
            pltpu.SemaphoreType.DMA((7,)),
        ],
        compiler_params=pltpu.CompilerParams(
            collective_id=0, has_side_effects=True, vmem_limit_bytes=56 << 20),
    )(cand, orbitals)


def local(orbitals, block_order):
    own_index = lax.axis_index("orb")
    local_cols = orbitals.shape[0]
    first_block = block_order[0]
    second_block = block_order[1]

    def candidate(block_index):
        piece = lax.dynamic_slice_in_dim(orbitals, block_index % BPD * B, B, 0)
        return jnp.where(block_index // BPD == own_index, piece, 0).astype(piece.dtype)

    cand = jnp.concatenate([candidate(first_block), candidate(second_block)], 0)
    panel, gram, diag = gram_sums(cand, orbitals)
    scale = jnp.float32(1.0 / CELLS)
    mixing = inverse_factor(diag * scale)
    column_blocks = (own_index * local_cols + jnp.arange(local_cols, dtype=jnp.int32)) // B
    scaled = mixing * scale
    upper_first = jnp.dot(scaled[:B, :B], gram[:B], precision=lax.Precision.HIGH)
    upper_second = jnp.dot(scaled[B:], gram, precision=lax.Precision.HIGH)
    upper_second = jnp.where((column_blocks == first_block)[None, :], jnp.float32(0.0), upper_second)
    factor_rows = jnp.concatenate([upper_first, upper_second], 0)
    rows_dev = ROWS // lax.axis_size("orb")
    mixing_rows = lax.dynamic_slice_in_dim(mixing, own_index * rows_dev, rows_dev, 0)
    high = lax.reduce_precision(mixing_rows, 8, 7)
    low = (mixing_rows - high).astype(jnp.bfloat16)
    ortho = jnp.dot(high.astype(jnp.bfloat16), panel, preferred_element_type=jnp.float32) + jnp.dot(
        low, panel, preferred_element_type=jnp.float32)
    return (factor_rows, ortho)


def solution(mesh):
    return jax.shard_map(
        local,
        mesh=mesh,
        in_specs=(P("orb", "grid"), P()),
        out_specs=(P(None, "orb"), P("orb", "grid")),
        check_vma=False,
    )
```

```python
import jax
import jax.numpy as jnp
from jax import lax
from jax.experimental import pallas as pl
from jax.experimental.pallas import tpu as pltpu
from jax.sharding import PartitionSpec as P

B = 512
BPD = 4
BLK = 128
SUB = 8
HI = lax.Precision.HIGHEST


def invert_block(block_ref, out_ref, hook):
    shape = (SUB, BLK)
    lane = lax.broadcasted_iota(jnp.int32, shape, 1)
    row = lax.broadcasted_iota(jnp.int32, shape, 0)
    count = BLK // SUB
    tiles = [block_ref[SUB * i : SUB * i + SUB, :] for i in range(count)]
    for c in range(count):
        hook(c)
        low = SUB * c
        here = jnp.logical_and(lane >= low, lane < low + SUB)
        pivot = tiles[c]
        column = [jnp.broadcast_to(pivot[:, low + m : low + m + 1], shape) for m in range(SUB)]
        a = {}
        for m in range(SUB):
            for i in range(m, SUB):
                a[i, m] = jnp.broadcast_to(column[m][i : i + 1, :], shape)
        marked = jnp.where(here, (lane - low == row).astype(jnp.float32), pivot)
        y = [jnp.broadcast_to(marked[k : k + 1, :], shape) for k in range(SUB)]
        t = {}
        for m in range(SUB):
            r = lax.rsqrt(a[m, m])
            for i in range(m + 1, SUB):
                a[i, m] = a[i, m] * r
            y[m] = y[m] * r
            for k in range(m):
                t[m, k] = t[m, k] * r
            t[m, m] = r
            for j in range(m + 1, SUB):
                for i in range(j, SUB):
                    a[i, j] = a[i, j] - a[i, m] * a[j, m]
            for i in range(m + 1, SUB):
                y[i] = y[i] - a[i, m] * y[m]
                for k in range(m):
                    t[i, k] = t[i, k] - a[i, m] * t[m, k]
                t[i, m] = -(a[i, m] * r)
        tile = y[0]
        for i in range(1, SUB):
            tile = jnp.where(row == i, y[i], tile)
        out_ref[low : low + SUB, :] = jnp.where(lane < low + SUB, tile, 0.0)
        if c == count - 1:
            break
        z = []
        for k in range(SUB):
            acc = t[k, k] * y[k]
            for i in range(k + 1, SUB):
                acc = acc + t[i, k] * y[i]
            z.append(acc)
        for r in range(c + 1, count):
            terms = [jnp.broadcast_to(tiles[r][:, low + m : low + m + 1], shape) * z[m] for m in range(SUB)]
            while len(terms) > 1:
                terms = [terms[i] + terms[i + 1] for i in range(0, len(terms), 2)]
            tiles[r] = jnp.where(here, 0.0, tiles[r]) - terms[0]


ROWS = 2 * B
LOCAL = 2048
WIDE = 1024
RING = 4
PIECES = 2
PIECE = B // 2 // PIECES
CELLS = 49152
MESH = pl.DeviceIdType.MESH
UNIT_SHAPES = ((256, 256), (512, 256), (512, 1024), (512, 1024))
COPIES = 22


def remote(src, dst, send, recv, axis, other):
    return pltpu.make_async_remote_copy(
        src_ref=src, dst_ref=dst, send_sem=send, recv_sem=recv, device_id={axis: other}, device_id_type=MESH)


class HalfReduce:
    def __init__(self, data, first, second, third, send, recv, free, p, p_next, p_prev, q, q_next, q_prev, y, y_mate):
        self.data, self.first, self.second, self.third, self.free = data, first, second, third, free
        self.p_ring, self.q_ring = (p_next, p_prev), (q_next, q_prev)
        size = data.shape[0]
        one, two, three = size // 4, size // 16, size // 32
        base = p * one
        low = base + q * two
        count = iter(range(COPIES))

        def make(src, dst, other):
            i = next(count)
            return remote(src, dst, send.at[i], recv.at[i], "grid", other)

        def cut(start, pos, length):
            half = length // 2
            return lambda turn, which: pl.ds(
                pl.multiple_of(start + ((pos + turn) % RING) * length + which * half, 8), half)

        def reduce_copies(rows, slots, following, previous):
            return [
                make(data.at[rows[2, 0]], slots.at[0], following),
                make(data.at[rows[2, 1]], slots.at[1], previous),
                make(data.at[rows[1, 1]], slots.at[2], following),
                make(data.at[rows[3, 0]], slots.at[3], previous),
                make(slots.at[0], slots.at[4], following),
                make(slots.at[1], slots.at[5], previous),
            ]

        def gather_copies(rows, own, following, previous):
            return [
                make(data.at[own], data.at[own], following),
                make(data.at[own], data.at[own], previous),
                make(data.at[rows[3, 0]], data.at[rows[3, 0]], following),
                make(data.at[rows[1, 1]], data.at[rows[1, 1]], previous),
            ]

        cut_p, cut_q = cut(0, p, one), cut(base, q, two)
        self.rows_p = {(t, w): cut_p(t, w) for t in range(RING) for w in range(2)}
        self.rows_q = {(t, w): cut_q(t, w) for t in range(RING) for w in range(2)}
        own_p = pl.ds(pl.multiple_of(base, 8), one)
        own_q = pl.ds(pl.multiple_of(low, 8), two)
        self.own_y = pl.ds(pl.multiple_of(low + y * three, 8), three)
        self.rest_y = pl.ds(pl.multiple_of(low + (1 - y) * three, 8), three)
        self.reduce_p = reduce_copies(self.rows_p, first, p_next, p_prev)
        self.reduce_q = reduce_copies(self.rows_q, second, q_next, q_prev)
        self.swap = make(data.at[self.rest_y], third.at[0], y_mate)
        self.share = make(data.at[self.own_y], third.at[1], y_mate)
        self.gather_q = gather_copies(self.rows_q, own_q, q_next, q_prev)
        self.gather_p = gather_copies(self.rows_p, own_p, p_next, p_prev)

    def begin(self, copies):
        for copy in copies[:4]:
            copy.start()

    def middle(self, copies, rows, slots):
        copies[0].wait_recv()
        slots[0] = slots[0] + self.data[rows[1, 0], :]
        copies[4].start()
        copies[1].wait_recv()
        slots[1] = slots[1] + self.data[rows[3, 1], :]
        copies[5].start()

    def end(self, copies, rows, slots, ring, free):
        copies[2].wait_recv()
        copies[3].wait_recv()
        copies[4].wait_recv()
        self.data[rows[0, 0], :] = self.data[rows[0, 0], :] + (slots[3] + slots[4])
        copies[5].wait_recv()
        self.data[rows[0, 1], :] = self.data[rows[0, 1], :] + (slots[2] + slots[5])
        for copy in copies:
            copy.wait_send()
        for other in ring:
            pl.semaphore_signal(free, inc=1, device_id={"grid": other}, device_id_type=MESH)

    def spread(self, copies, free):
        pl.semaphore_wait(free, 2)
        copies[0].start()
        copies[1].start()

    def forward(self, copies):
        copies[0].wait_recv()
        copies[2].start()
        copies[1].wait_recv()
        copies[3].start()

    def settle(self, copies):
        copies[2].wait_recv()
        copies[3].wait_recv()
        for copy in copies:
            copy.wait_send()

    def step(self, i):
        p, q = self.reduce_p, self.reduce_q
        if i == 0:
            self.begin(p)
        elif i == 1:
            self.middle(p, self.rows_p, self.first)
        elif i == 2:
            self.end(p, self.rows_p, self.first, self.p_ring, self.free.at[0])
            self.begin(q)
        elif i == 3:
            self.middle(q, self.rows_q, self.second)
        elif i == 4:
            self.end(q, self.rows_q, self.second, self.q_ring, self.free.at[1])
            self.swap.start()
        elif i == 5:
            self.swap.wait_recv()
            self.data[self.own_y, :] = self.data[self.own_y, :] + self.third[0]
            self.share.start()
        elif i == 6:
            self.share.wait_recv()
            self.swap.wait_send()
            self.share.wait_send()
            self.data[self.rest_y, :] = self.third[1]
            self.spread(self.gather_q, self.free.at[1])
        elif i == 7:
            self.forward(self.gather_q)
        elif i == 8:
            self.settle(self.gather_q)
            self.spread(self.gather_p, self.free.at[0])
        elif i == 9:
            self.forward(self.gather_p)
        elif i == 10:
            self.settle(self.gather_p)


STEPS = 11


def whole_kernel(cand_ref, orb_ref, panel_out, gram_out, mixing_out,
                 panel, merged, from_core, from_chip, tiles_a, tiles_b, main, mate_a, mate_b,
                 s00, s01, s02, s10, s11, s12, s20, s21, s22, s30, s31, s32,
                 work, block, inv, coupling, mixing,
                 panel_send, panel_recv, send, recv, free, local_sem):
    o = lax.axis_index("orb")
    g = lax.axis_index("grid")
    core = o % 2
    mate = o + 1 - 2 * core
    across = (o + 2) % 4
    x = g // 8
    y = (g // 4) % 2
    z = g % 4
    x_next = ((x + 1) % RING) * 8 + y * 4 + z
    x_prev = ((x + 3) % RING) * 8 + y * 4 + z
    z_next = x * 8 + y * 4 + (z + 1) % RING
    z_prev = x * 8 + y * 4 + (z + 3) % RING
    y_mate = x * 8 + (1 - y) * 4 + z

    barrier = pltpu.get_barrier_semaphore()
    for other in (mate, across):
        pl.semaphore_signal(barrier, inc=1, device_id={"orb": other}, device_id_type=MESH)
    for other in (x_next, x_prev, z_next, z_prev, y_mate):
        pl.semaphore_signal(barrier, inc=1, device_id={"grid": other}, device_id_type=MESH)
    pl.semaphore_wait(barrier, 7)

    data = ([tiles_a.at[0], tiles_a.at[1]], [tiles_b.at[0], tiles_b.at[1]],
            [main.at[0, 0], main.at[0, 1]], [main.at[1, 0], main.at[1, 1]])
    slots = ((s00, s01, s02), (s10, s11, s12), (s20, s21, s22), (s30, s31, s32))
    units = []
    for u in range(4):
        first, second, third = slots[u]
        units.append([
            HalfReduce(data[u][0], first.at[0], second.at[0], third.at[0], send.at[u, 0], recv.at[u, 0],
                       free.at[u, 0], x, x_next, x_prev, z, z_next, z_prev, y, y_mate),
            HalfReduce(data[u][1], first.at[1], second.at[1], third.at[1], send.at[u, 1], recv.at[u, 1],
                       free.at[u, 1], z, z_next, z_prev, x, x_next, x_prev, y, y_mate),
        ])
    done = [0] * 4

    def advance(u, upto=None):
        upto = done[u] + 1 if upto is None else upto
        while done[u] < upto:
            for half in units[u]:
                half.step(done[u])
            done[u] += 1

    quarter = B // 2

    def part(t, which, j):
        return pl.ds(pl.multiple_of(t * B + which * quarter + j * PIECE, PIECE), PIECE)

    def orb_copy(src, dst, other, i):
        return remote(src, dst, panel_send.at[i], panel_recv.at[i], "orb", other)

    pieces = [(t, j) for t in range(2) for j in range(PIECES)]
    mine = {tj: part(tj[0], core, tj[1]) for tj in pieces}
    theirs = {tj: part(tj[0], 1 - core, tj[1]) for tj in pieces}
    n = len(pieces)
    give = {tj: orb_copy(cand_ref.at[theirs[tj]], from_core.at[i], mate, i) for i, tj in enumerate(pieces)}
    cross = {tj: orb_copy(merged.at[i], from_chip.at[i], across, n + i) for i, tj in enumerate(pieces)}
    share = {tj: orb_copy(panel.at[mine[tj]], panel.at[mine[tj]], mate, 2 * n + i) for i, tj in enumerate(pieces)}
    for tj in pieces:
        give[tj].start()
    for i, tj in enumerate(pieces):
        give[tj].wait_recv()
        merged[i] = cand_ref[mine[tj], :] + from_core[i]
        cross[tj].start()

    def collect(t):
        for j in range(PIECES):
            i = pieces.index((t, j))
            cross[t, j].wait_recv()
            panel[mine[t, j], :] = merged[i] + from_chip[i]
            share[t, j].start()

    def receive(t):
        for j in range(PIECES):
            share[t, j].wait_recv()

    contract = (((1,), (1,)), ((), ()))

    def product(rows, columns):
        return lax.dot_general(rows, columns, contract, preferred_element_type=jnp.float32)

    def core_rows(t):
        return panel[pl.ds(pl.multiple_of(t * B + core * quarter, quarter), quarter), :]

    def main_gram(t):
        for h in range(2):
            def column(i, carry, h=h):
                at = pl.multiple_of(i * 256, 256)
                main[t, h, :, pl.ds(at, 256)] = product(
                    panel[t * B : (t + 1) * B, :], orb_ref[pl.ds(h * WIDE + at, 256), :])
                return carry

            lax.fori_loop(0, WIDE // 256, column, 0)

    collect(0)
    receive(0)
    for h in range(2):
        tiles_a[h] = product(core_rows(0), panel[h * quarter : (h + 1) * quarter, :])
    advance(0)
    main_gram(0)
    advance(0)
    advance(2)
    collect(1)
    advance(0)
    advance(0)
    receive(1)
    advance(0)
    for h in range(2):
        columns = panel[B + h * quarter : B + (h + 1) * quarter, :]
        tiles_b[h, :quarter, :] = product(core_rows(0), columns)
        tiles_b[h, quarter:, :] = product(core_rows(1), columns)
    advance(0)
    advance(1)
    advance(0)
    main_gram(1)
    advance(0)
    advance(0)
    advance(0)
    advance(0)
    advance(2)
    save_panel = pltpu.make_async_copy(panel, panel_out, local_sem.at[0])
    save_panel.start()

    share_a = [orb_copy(tiles_a.at[h], mate_a.at[h], mate, 3 * n + h) for h in range(2)]
    share_b = [orb_copy(tiles_b.at[h], mate_b.at[h], mate, 3 * n + 2 + h) for h in range(2)]
    scale = 1.0 / CELLS
    own_rows = pl.ds(pl.multiple_of(core * quarter, quarter), quarter)
    mate_rows = pl.ds(pl.multiple_of((1 - core) * quarter, quarter), quarter)
    for copy in share_a:
        copy.start()
    for h in range(2):
        columns = slice(h * quarter, (h + 1) * quarter)
        work[own_rows, columns] = tiles_a[h] * scale
        share_a[h].wait_recv()
        work[mate_rows, columns] = mate_a[h] * scale

    def factor(phase, hooks):
        column = lax.broadcasted_iota(jnp.int32, (BLK, B), 1)
        low = phase * B

        def step(k, carry):
            start = pl.multiple_of(k * BLK, BLK)
            here = pl.ds(start, BLK)
            block[...] = work[here, here]

            def hook(c):
                for i in range(B // BLK):
                    if (i, c) in hooks:
                        pl.when(k == i)(hooks[i, c])

            invert_block(block, inv, hook)
            t = inv[...]
            row = jnp.dot(t, work[here, :], precision=HI, preferred_element_type=jnp.float32)
            mixing[pl.ds(low + start, BLK), low : low + B] = jnp.where(column < start, row, 0.0)
            mixing[pl.ds(low + start, BLK), pl.ds(low + start, BLK)] = t
            work[here, :] = row
            work[here, here] = t

            def update(i, carry):
                rows = pl.ds(pl.multiple_of(i * BLK, BLK), BLK)
                u = work[here, rows]
                work[rows, here] = jnp.zeros((BLK, BLK), jnp.float32)
                work[rows, :] -= lax.dot_general(
                    u, work[here, :], (((0,), (0,)), ((), ())), precision=HI, preferred_element_type=jnp.float32)
                return carry

            return lax.fori_loop(k + 1, B // BLK, update, carry)

        lax.fori_loop(0, B // BLK, step, 0)

    def schedule(order):
        hooks = {}
        spots = [(k, c) for k in range(B // BLK) for c in (0, 4, 8, 12)]
        for spot, names in zip(spots, order):
            todo = []
            for u in names:
                if done[u] < STEPS:
                    todo += [(half, done[u]) for half in units[u]]
                    done[u] += 1
            if todo:
                hooks[spot] = lambda todo=todo: [half.step(i) for half, i in todo] and None
        return hooks

    factor(0, schedule(ORDER_A))
    for copy in share_b:
        copy.start()
    for h in range(2):
        columns = slice(h * quarter, (h + 1) * quarter)
        coupling[own_rows, columns] = tiles_b[h, :quarter, :] * scale
        work[own_rows, columns] = tiles_b[h, quarter:, :] * scale
        share_b[h].wait_recv()
        coupling[mate_rows, columns] = mate_b[h, :quarter, :] * scale
        work[mate_rows, columns] = mate_b[h, quarter:, :] * scale
    mixing[:B, B:] = jnp.zeros((B, B), jnp.float32)
    first = mixing[:B, :B]
    coupling[...] = jnp.dot(first, coupling[...], precision=HI, preferred_element_type=jnp.float32)
    turned = (((0,), (0,)), ((), ()))
    work[...] -= lax.dot_general(
        coupling[...], coupling[...], turned, precision=HI, preferred_element_type=jnp.float32)
    coupling[...] = lax.dot_general(
        coupling[...], mixing[:B, :B], turned, precision=HI, preferred_element_type=jnp.float32)
    factor(1, schedule(ORDER_B))
    mixing[B:, :B] = -jnp.dot(mixing[B:, B:], coupling[...], precision=HI, preferred_element_type=jnp.float32)
    save_mixing = pltpu.make_async_copy(mixing, mixing_out, local_sem.at[1])
    save_mixing.start()
    saves = [save_panel, save_mixing]
    while done[2] < STEPS or done[3] < STEPS:
        for u in (2, 3):
            if done[u] < STEPS:
                advance(u)
    for t in range(2):
        for h in range(2):
            saves.append(pltpu.make_async_copy(
                main.at[t, h], gram_out.at[pl.ds(t * B, B), pl.ds(h * WIDE, WIDE)], local_sem.at[2 + 2 * t + h]))
            saves[-1].start()
    for copy in [*give.values(), *cross.values(), *share.values(), *share_a, *share_b]:
        copy.wait_send()
    for save in saves:
        save.wait()


ORDER_A = [(1,), (1,), (2,), (3,), (1,), (1,), (2,), (3,), (1,), (1,), (2,), (1,), (3,), (1,), (1,), (1,)]
ORDER_B = [(2,), (3,), (2,), (3,), (2,), (3,), (2,), (3,), (2,), (3,), (2,), (3,), (2,), (3,), (2,), (3,)]


def whole(cand, orbitals):
    cells = orbitals.shape[1]
    f32 = jnp.float32
    bf16 = jnp.bfloat16
    any_space = pl.BlockSpec(memory_space=pl.ANY)
    n = 2 * PIECES
    slots = []
    for rows, columns in UNIT_SHAPES:
        slots += [
            pltpu.VMEM((2, 6, rows // 8, columns), f32),
            pltpu.VMEM((2, 6, rows // 32, columns), f32),
            pltpu.VMEM((2, 2, rows // 32, columns), f32),
        ]
    return pl.pallas_call(
        whole_kernel,
        out_shape=(
            jax.ShapeDtypeStruct((ROWS, cells), bf16),
            jax.ShapeDtypeStruct((ROWS, LOCAL), f32),
            jax.ShapeDtypeStruct((ROWS, ROWS), f32),
        ),
        in_specs=[pl.BlockSpec(memory_space=pltpu.VMEM)] * 2,
        out_specs=(any_space,) * 3,
        scratch_shapes=[
            pltpu.VMEM((ROWS, cells), bf16),
            pltpu.VMEM((n, PIECE, cells), bf16),
            pltpu.VMEM((n, PIECE, cells), bf16),
            pltpu.VMEM((n, PIECE, cells), bf16),
            pltpu.VMEM((2, 256, 256), f32),
            pltpu.VMEM((2, 512, 256), f32),
            pltpu.VMEM((2, 2, B, WIDE), f32),
            pltpu.VMEM((2, 256, 256), f32),
            pltpu.VMEM((2, 512, 256), f32),
            *slots,
            pltpu.VMEM((B, B), f32),
            pltpu.VMEM((BLK, BLK), f32),
            pltpu.VMEM((BLK, BLK), f32),
            pltpu.VMEM((B, B), f32),
            pltpu.VMEM((ROWS, ROWS), f32),
            pltpu.SemaphoreType.DMA((3 * n + 4,)),
            pltpu.SemaphoreType.DMA((3 * n + 4,)),
            pltpu.SemaphoreType.DMA((4, 2, COPIES)),
            pltpu.SemaphoreType.DMA((4, 2, COPIES)),
            pltpu.SemaphoreType.REGULAR((4, 2, 2)),
            pltpu.SemaphoreType.DMA((6,)),
        ],
        compiler_params=pltpu.CompilerParams(
            collective_id=0, has_side_effects=True, vmem_limit_bytes=60 << 20),
    )(cand, orbitals)


def local(orbitals, block_order):
    own_index = lax.axis_index("orb")
    local_cols = orbitals.shape[0]
    first_block = block_order[0]
    second_block = block_order[1]

    def candidate(block_index):
        piece = lax.dynamic_slice_in_dim(orbitals, block_index % BPD * B, B, 0)
        return jnp.where(block_index // BPD == own_index, piece, 0).astype(piece.dtype)

    cand = jnp.concatenate([candidate(first_block), candidate(second_block)], 0)
    panel, gram, mixing = whole(cand, orbitals)
    scale = jnp.float32(1.0 / CELLS)
    column_blocks = (own_index * local_cols + jnp.arange(local_cols, dtype=jnp.int32)) // B
    scaled = mixing * scale
    upper_first = jnp.dot(scaled[:B, :B], gram[:B], precision=lax.Precision.HIGH)
    upper_second = jnp.dot(scaled[B:], gram, precision=lax.Precision.HIGH)
    upper_second = jnp.where((column_blocks == first_block)[None, :], jnp.float32(0.0), upper_second)
    factor_rows = jnp.concatenate([upper_first, upper_second], 0)
    rows_dev = ROWS // lax.axis_size("orb")
    mixing_rows = lax.dynamic_slice_in_dim(mixing, own_index * rows_dev, rows_dev, 0)
    high = lax.reduce_precision(mixing_rows, 8, 7)
    low = (mixing_rows - high).astype(jnp.bfloat16)
    ortho = jnp.dot(high.astype(jnp.bfloat16), panel, preferred_element_type=jnp.float32) + jnp.dot(
        low, panel, preferred_element_type=jnp.float32)
    return (factor_rows, ortho)


def solution(mesh):
    return jax.shard_map(
        local,
        mesh=mesh,
        in_specs=(P("orb", "grid"), P()),
        out_specs=(P(None, "orb"), P("orb", "grid")),
        check_vma=False,
    )
```

```python
import jax
import jax.numpy as jnp
from jax import lax
from jax.experimental import pallas as pl
from jax.experimental.pallas import tpu as pltpu
from jax.sharding import PartitionSpec as P

B = 512
BPD = 4
BLK = 128
SUB = 8
HI = lax.Precision.HIGHEST


def invert_block(block_ref, out_ref, hook):
    shape = (SUB, BLK)
    lane = lax.broadcasted_iota(jnp.int32, shape, 1)
    row = lax.broadcasted_iota(jnp.int32, shape, 0)
    count = BLK // SUB
    tiles = [block_ref[SUB * i : SUB * i + SUB, :] for i in range(count)]
    for c in range(count):
        hook(c)
        low = SUB * c
        here = jnp.logical_and(lane >= low, lane < low + SUB)
        pivot = tiles[c]
        column = [jnp.broadcast_to(pivot[:, low + m : low + m + 1], shape) for m in range(SUB)]
        a = {}
        for m in range(SUB):
            for i in range(m, SUB):
                a[i, m] = jnp.broadcast_to(column[m][i : i + 1, :], shape)
        marked = jnp.where(here, (lane - low == row).astype(jnp.float32), pivot)
        y = [jnp.broadcast_to(marked[k : k + 1, :], shape) for k in range(SUB)]
        t = {}
        for m in range(SUB):
            r = lax.rsqrt(a[m, m])
            for i in range(m + 1, SUB):
                a[i, m] = a[i, m] * r
            y[m] = y[m] * r
            for k in range(m):
                t[m, k] = t[m, k] * r
            t[m, m] = r
            for j in range(m + 1, SUB):
                for i in range(j, SUB):
                    a[i, j] = a[i, j] - a[i, m] * a[j, m]
            for i in range(m + 1, SUB):
                y[i] = y[i] - a[i, m] * y[m]
                for k in range(m):
                    t[i, k] = t[i, k] - a[i, m] * t[m, k]
                t[i, m] = -(a[i, m] * r)
        tile = y[0]
        for i in range(1, SUB):
            tile = jnp.where(row == i, y[i], tile)
        out_ref[low : low + SUB, :] = jnp.where(lane < low + SUB, tile, 0.0)
        if c == count - 1:
            break
        z = []
        for k in range(SUB):
            acc = t[k, k] * y[k]
            for i in range(k + 1, SUB):
                acc = acc + t[i, k] * y[i]
            z.append(acc)
        for r in range(c + 1, count):
            terms = [jnp.broadcast_to(tiles[r][:, low + m : low + m + 1], shape) * z[m] for m in range(SUB)]
            while len(terms) > 1:
                terms = [terms[i] + terms[i + 1] for i in range(0, len(terms), 2)]
            tiles[r] = jnp.where(here, 0.0, tiles[r]) - terms[0]


ROWS = 2 * B
LOCAL = 2048
WIDE = 1024
RING = 4
PIECES = 2
PIECE = B // 2 // PIECES
CELLS = 49152
MESH = pl.DeviceIdType.MESH
UNIT_SHAPES = ((256, 256), (512, 256)) + ((256, 1024),) * 4
COPIES = 24
PEERS = [(turn, flip) for turn in range(RING) for flip in range(2)][1:]


def remote(src, dst, send, recv, axis, other):
    return pltpu.make_async_remote_copy(
        src_ref=src, dst_ref=dst, send_sem=send, recv_sem=recv, device_id={axis: other}, device_id_type=MESH)


class RingReduce:
    steps = 11

    def __init__(self, data, first, second, third, send, recv, free, p, p_next, p_prev, q, q_next, q_prev, y, device):
        y_mate = device(q, 1 - y)
        self.data, self.first, self.second, self.third, self.free = data, first, second, third, free
        self.p_ring, self.q_ring = (p_next, p_prev), (q_next, q_prev)
        size = data.shape[0]
        one, two, three = size // 4, size // 16, size // 32
        base = p * one
        low = base + q * two
        count = iter(range(COPIES))

        def make(src, dst, other):
            i = next(count)
            return remote(src, dst, send.at[i], recv.at[i], "grid", other)

        def cut(start, pos, length):
            half = length // 2
            return lambda turn, which: pl.ds(
                pl.multiple_of(start + ((pos + turn) % RING) * length + which * half, 8), half)

        def reduce_copies(rows, slots, following, previous):
            return [
                make(data.at[rows[2, 0]], slots.at[0], following),
                make(data.at[rows[2, 1]], slots.at[1], previous),
                make(data.at[rows[1, 1]], slots.at[2], following),
                make(data.at[rows[3, 0]], slots.at[3], previous),
                make(slots.at[0], slots.at[4], following),
                make(slots.at[1], slots.at[5], previous),
            ]

        def gather_copies(rows, own, following, previous):
            return [
                make(data.at[own], data.at[own], following),
                make(data.at[own], data.at[own], previous),
                make(data.at[rows[3, 0]], data.at[rows[3, 0]], following),
                make(data.at[rows[1, 1]], data.at[rows[1, 1]], previous),
            ]

        cut_p, cut_q = cut(0, p, one), cut(base, q, two)
        self.rows_p = {(t, w): cut_p(t, w) for t in range(RING) for w in range(2)}
        self.rows_q = {(t, w): cut_q(t, w) for t in range(RING) for w in range(2)}
        own_p = pl.ds(pl.multiple_of(base, 8), one)
        own_q = pl.ds(pl.multiple_of(low, 8), two)
        self.own_y = pl.ds(pl.multiple_of(low + y * three, 8), three)
        self.rest_y = pl.ds(pl.multiple_of(low + (1 - y) * three, 8), three)
        self.reduce_p = reduce_copies(self.rows_p, first, p_next, p_prev)
        self.reduce_q = reduce_copies(self.rows_q, second, q_next, q_prev)
        self.swap = make(data.at[self.rest_y], third.at[0], y_mate)
        self.share = make(data.at[self.own_y], third.at[1], y_mate)
        self.gather_q = gather_copies(self.rows_q, own_q, q_next, q_prev)
        self.gather_p = gather_copies(self.rows_p, own_p, p_next, p_prev)

    def begin(self, copies):
        for copy in copies[:4]:
            copy.start()

    def middle(self, copies, rows, slots):
        copies[0].wait_recv()
        slots[0] = slots[0] + self.data[rows[1, 0], :]
        copies[4].start()
        copies[1].wait_recv()
        slots[1] = slots[1] + self.data[rows[3, 1], :]
        copies[5].start()

    def end(self, copies, rows, slots, ring, free):
        copies[2].wait_recv()
        copies[3].wait_recv()
        copies[4].wait_recv()
        self.data[rows[0, 0], :] = self.data[rows[0, 0], :] + (slots[3] + slots[4])
        copies[5].wait_recv()
        self.data[rows[0, 1], :] = self.data[rows[0, 1], :] + (slots[2] + slots[5])
        for copy in copies:
            copy.wait_send()
        for other in ring:
            pl.semaphore_signal(free, inc=1, device_id={"grid": other}, device_id_type=MESH)

    def spread(self, copies, free):
        pl.semaphore_wait(free, 2)
        copies[0].start()
        copies[1].start()

    def forward(self, copies):
        copies[0].wait_recv()
        copies[2].start()
        copies[1].wait_recv()
        copies[3].start()

    def settle(self, copies):
        copies[2].wait_recv()
        copies[3].wait_recv()
        for copy in copies:
            copy.wait_send()

    def step(self, i):
        p, q = self.reduce_p, self.reduce_q
        if i == 0:
            self.begin(p)
        elif i == 1:
            self.middle(p, self.rows_p, self.first)
        elif i == 2:
            self.end(p, self.rows_p, self.first, self.p_ring, self.free.at[0])
            self.begin(q)
        elif i == 3:
            self.middle(q, self.rows_q, self.second)
        elif i == 4:
            self.end(q, self.rows_q, self.second, self.q_ring, self.free.at[1])
            self.swap.start()
        elif i == 5:
            self.swap.wait_recv()
            self.data[self.own_y, :] = self.data[self.own_y, :] + self.third[0]
            self.share.start()
        elif i == 6:
            self.share.wait_recv()
            self.swap.wait_send()
            self.share.wait_send()
            self.data[self.rest_y, :] = self.third[1]
            self.spread(self.gather_q, self.free.at[1])
        elif i == 7:
            self.forward(self.gather_q)
        elif i == 8:
            self.settle(self.gather_q)
            self.spread(self.gather_p, self.free.at[0])
        elif i == 9:
            self.forward(self.gather_p)
        elif i == 10:
            self.settle(self.gather_p)


class DirectReduce(RingReduce):
    steps = 7

    def __init__(self, data, first, second, third, send, recv, free, p, p_next, p_prev, q, q_next, q_prev, y, device):
        self.data, self.first, self.second, self.free = data, first, second, free
        self.p_ring = (p_next, p_prev)
        size = data.shape[0]
        one, three = size // 4, size // 32
        half = one // 2
        base = p * one
        count = iter(range(COPIES))

        def make(src, dst, other):
            i = next(count)
            return remote(src, dst, send.at[i], recv.at[i], "grid", other)

        def rows(turn, which):
            return pl.ds(pl.multiple_of(((p + turn) % RING) * one + which * half, 8), half)

        def member(turn, flip):
            return pl.ds(pl.multiple_of(base + (((q + turn) % RING) * 2 + (y + flip) % 2) * three, 8), three)

        self.rows_p = {(t, w): rows(t, w) for t in range(RING) for w in range(2)}
        self.own = member(0, 0)
        self.origin = [member(RING - turn, flip) for turn, flip in PEERS]
        own_p = pl.ds(pl.multiple_of(base, 8), one)
        others = [device((q + turn) % RING, (y + flip) % 2) for turn, flip in PEERS]
        r = self.rows_p
        self.reduce_p = [
            make(data.at[r[2, 0]], first.at[0], p_next),
            make(data.at[r[2, 1]], first.at[1], p_prev),
            make(data.at[r[1, 1]], first.at[2], p_next),
            make(data.at[r[3, 0]], first.at[3], p_prev),
            make(first.at[0], first.at[4], p_next),
            make(first.at[1], first.at[5], p_prev),
        ]
        self.scatter = [make(data.at[member(*peer)], second.at[i], others[i]) for i, peer in enumerate(PEERS)]
        self.share = [make(data.at[self.own], second.at[7 + i], others[i]) for i in range(7)]
        self.gather_p = [
            make(data.at[own_p], data.at[own_p], p_next),
            make(data.at[own_p], data.at[own_p], p_prev),
            make(data.at[r[3, 0]], data.at[r[3, 0]], p_next),
            make(data.at[r[1, 1]], data.at[r[1, 1]], p_prev),
        ]

    def step(self, i):
        p = self.reduce_p
        if i == 0:
            self.begin(p)
        elif i == 1:
            self.middle(p, self.rows_p, self.first)
        elif i == 2:
            self.end(p, self.rows_p, self.first, self.p_ring, self.free.at[0])
            for copy in self.scatter:
                copy.start()
        elif i == 3:
            total = self.data[self.own, :]
            for j, copy in enumerate(self.scatter):
                copy.wait_recv()
                total = total + self.second[j]
            self.data[self.own, :] = total
            for copy in self.share:
                copy.start()
        elif i == 4:
            for copy in self.scatter:
                copy.wait_send()
            for j, copy in enumerate(self.share):
                copy.wait_recv()
                self.data[self.origin[j], :] = self.second[7 + j]
            for copy in self.share:
                copy.wait_send()
            self.spread(self.gather_p, self.free.at[0])
        elif i == 5:
            self.forward(self.gather_p)
        elif i == 6:
            self.settle(self.gather_p)


def whole_kernel(cand_ref, orb_ref, panel_out, gram_out, mixing_out,
                 panel, merged, from_core, from_chip, tiles_a, tiles_b, main, mate_a, mate_b,
                 *rest):
    slots = [rest[3 * u : 3 * u + 3] for u in range(6)]
    work, block, inv, coupling, mixing, panel_send, panel_recv, send, recv, free, local_sem = rest[18:]
    o = lax.axis_index("orb")
    g = lax.axis_index("grid")
    core = o % 2
    mate = o + 1 - 2 * core
    across = (o + 2) % 4
    x = g // 8
    y = (g // 4) % 2
    z = g % 4
    x_next = ((x + 1) % RING) * 8 + y * 4 + z
    x_prev = ((x + 3) % RING) * 8 + y * 4 + z
    z_next = x * 8 + y * 4 + (z + 1) % RING
    z_prev = x * 8 + y * 4 + (z + 3) % RING

    def at_z(q, flip):
        return x * 8 + flip * 4 + q

    def at_x(q, flip):
        return q * 8 + flip * 4 + z

    barrier = pltpu.get_barrier_semaphore()
    near = [mate, across]
    for other in near:
        pl.semaphore_signal(barrier, inc=1, device_id={"orb": other}, device_id_type=MESH)
    far = [at_z((z + turn) % RING, (y + flip) % 2) for turn, flip in PEERS]
    far += [at_x((x + turn) % RING, (y + flip) % 2) for turn, flip in PEERS if turn]
    for other in far:
        pl.semaphore_signal(barrier, inc=1, device_id={"grid": other}, device_id_type=MESH)
    pl.semaphore_wait(barrier, len(near) + len(far))

    data = [[tiles_a.at[0], tiles_a.at[1]], [tiles_b.at[0], tiles_b.at[1]]]
    data += [[main.at[i, 0], main.at[i, 1]] for i in range(4)]
    units = []
    for u in range(6):
        kind = DirectReduce if u < 2 else RingReduce
        first, second, third = slots[u]
        units.append([
            kind(data[u][0], first.at[0], second.at[0], third.at[0], send.at[u, 0], recv.at[u, 0],
                 free.at[u, 0], x, x_next, x_prev, z, z_next, z_prev, y, at_z),
            kind(data[u][1], first.at[1], second.at[1], third.at[1], send.at[u, 1], recv.at[u, 1],
                 free.at[u, 1], z, z_next, z_prev, x, x_next, x_prev, y, at_x),
        ])
    done = [0] * 6

    def advance(u):
        for half in units[u]:
            half.step(done[u])
        done[u] += 1

    quarter = B // 2

    def part(t, which, j):
        return pl.ds(pl.multiple_of(t * B + j * quarter + which * PIECE, PIECE), PIECE)

    def orb_copy(src, dst, other, i):
        return remote(src, dst, panel_send.at[i], panel_recv.at[i], "orb", other)

    pieces = [(t, j) for t in range(2) for j in range(PIECES)]
    mine = {tj: part(tj[0], core, tj[1]) for tj in pieces}
    theirs = {tj: part(tj[0], 1 - core, tj[1]) for tj in pieces}
    n = len(pieces)
    give = {tj: orb_copy(cand_ref.at[theirs[tj]], from_core.at[i], mate, i) for i, tj in enumerate(pieces)}
    cross = {tj: orb_copy(merged.at[i], from_chip.at[i], across, n + i) for i, tj in enumerate(pieces)}
    share = {tj: orb_copy(panel.at[mine[tj]], panel.at[mine[tj]], mate, 2 * n + i) for i, tj in enumerate(pieces)}
    for tj in pieces:
        give[tj].start()

    def merge(i):
        tj = pieces[i]
        give[tj].wait_recv()
        merged[i] = cand_ref[mine[tj], :] + from_core[i]
        cross[tj].start()

    def collect(i):
        tj = pieces[i]
        cross[tj].wait_recv()
        panel[mine[tj], :] = merged[i] + from_chip[i]
        share[tj].start()

    contract = (((1,), (1,)), ((), ()))

    def product(rows, columns):
        return lax.dot_general(rows, columns, contract, preferred_element_type=jnp.float32)

    def core_rows(t):
        return panel[pl.ds(pl.multiple_of(t * B + core * quarter, quarter), quarter), :]

    def main_gram(i):
        for h in range(2):
            def column(n, carry, h=h):
                at = pl.multiple_of(n * 256, 256)
                main[i, h, :, pl.ds(at, 256)] = product(
                    panel[i * quarter : (i + 1) * quarter, :], orb_ref[pl.ds(h * WIDE + at, 256), :])
                return carry

            lax.fori_loop(0, WIDE // 256, column, 0)

    def gram_a():
        for h in range(2):
            tiles_a[h] = product(core_rows(0), panel[h * quarter : (h + 1) * quarter, :])

    save_panel = pltpu.make_async_copy(panel, panel_out, local_sem.at[0])

    def gram_b():
        for h in range(2):
            columns = panel[B + h * quarter : B + (h + 1) * quarter, :]
            tiles_b[h, :quarter, :] = product(core_rows(0), columns)
            tiles_b[h, quarter:, :] = product(core_rows(1), columns)
        save_panel.start()

    share_a = [orb_copy(tiles_a.at[h], mate_a.at[h], mate, 3 * n + h) for h in range(2)]
    share_b = [orb_copy(tiles_b.at[h], mate_b.at[h], mate, 3 * n + 2 + h) for h in range(2)]
    scale = 1.0 / CELLS
    own_rows = pl.ds(pl.multiple_of(core * quarter, quarter), quarter)
    mate_rows = pl.ds(pl.multiple_of((1 - core) * quarter, quarter), quarter)

    def start_a():
        for copy in share_a:
            copy.start()

    def start_b():
        for copy in share_b:
            copy.start()

    def load_a():
        for h in range(2):
            columns = slice(h * quarter, (h + 1) * quarter)
            work[own_rows, columns] = tiles_a[h] * scale
            share_a[h].wait_recv()
            work[mate_rows, columns] = mate_a[h] * scale

    def action(name):
        kind, i = name[:-1], int(name[-1])
        if kind == "m" or kind == "d":
            u = 1 + i if kind == "m" else i - 1
            u = u + 1 if kind == "m" else u
            now = done[u]
            done[u] += 1
            return lambda: [half.step(now) for half in units[u]]
        table = {
            "gw": merge, "co": collect, "rc": lambda j: share[pieces[j]].wait_recv(), "g": main_gram,
            "a": lambda j: gram_a(), "b": lambda j: gram_b(), "xs": lambda j: start_a(),
            "xw": lambda j: load_a(), "ys": lambda j: start_b(),
        }
        return lambda: table[kind](i)

    def perform(names):
        for name in names:
            action(name)()

    def factor(phase, hooks):
        column = lax.broadcasted_iota(jnp.int32, (BLK, B), 1)
        low = phase * B

        def step(k, carry):
            start = pl.multiple_of(k * BLK, BLK)
            here = pl.ds(start, BLK)
            block[...] = work[here, here]

            def hook(c):
                for i in range(B // BLK):
                    if (i, c) in hooks:
                        pl.when(k == i)(hooks[i, c])

            invert_block(block, inv, hook)
            t = inv[...]
            row = jnp.dot(t, work[here, :], precision=HI, preferred_element_type=jnp.float32)
            mixing[pl.ds(low + start, BLK), low : low + B] = jnp.where(column < start, row, 0.0)
            mixing[pl.ds(low + start, BLK), pl.ds(low + start, BLK)] = t
            work[here, :] = row
            work[here, here] = t

            def update(i, carry):
                rows = pl.ds(pl.multiple_of(i * BLK, BLK), BLK)
                u = work[here, rows]
                work[rows, here] = jnp.zeros((BLK, BLK), jnp.float32)
                work[rows, :] -= lax.dot_general(
                    u, work[here, :], (((0,), (0,)), ((), ())), precision=HI, preferred_element_type=jnp.float32)
                return carry

            return lax.fori_loop(k + 1, B // BLK, update, carry)

        lax.fori_loop(0, B // BLK, step, 0)

    def hooks_of(phase):
        hooks = {}
        for (at, k, c), names in BETWEEN.items():
            if at == phase:
                todo = [action(name) for name in names]
                hooks[k, c] = lambda todo=todo: [do() for do in todo] and None
        return hooks

    perform(BEFORE)
    factor(0, hooks_of(0))
    perform(MIDDLE)
    for h in range(2):
        columns = slice(h * quarter, (h + 1) * quarter)
        coupling[own_rows, columns] = tiles_b[h, :quarter, :] * scale
        work[own_rows, columns] = tiles_b[h, quarter:, :] * scale
        share_b[h].wait_recv()
        coupling[mate_rows, columns] = mate_b[h, :quarter, :] * scale
        work[mate_rows, columns] = mate_b[h, quarter:, :] * scale
    mixing[:B, B:] = jnp.zeros((B, B), jnp.float32)
    first = mixing[:B, :B]
    coupling[...] = jnp.dot(first, coupling[...], precision=HI, preferred_element_type=jnp.float32)
    turned = (((0,), (0,)), ((), ()))
    work[...] -= lax.dot_general(
        coupling[...], coupling[...], turned, precision=HI, preferred_element_type=jnp.float32)
    coupling[...] = lax.dot_general(
        coupling[...], mixing[:B, :B], turned, precision=HI, preferred_element_type=jnp.float32)
    factor(1, hooks_of(1))
    mixing[B:, :B] = -jnp.dot(mixing[B:, B:], coupling[...], precision=HI, preferred_element_type=jnp.float32)
    save_mixing = pltpu.make_async_copy(mixing, mixing_out, local_sem.at[1])
    save_mixing.start()
    saves = [save_panel, save_mixing]
    perform(AFTER)
    for i in range(4):
        assert done[2 + i] == RingReduce.steps
        for h in range(2):
            saves.append(pltpu.make_async_copy(
                main.at[i, h], gram_out.at[pl.ds(i * quarter, quarter), pl.ds(h * WIDE, WIDE)],
                local_sem.at[2 + 2 * i + h]))
            saves[-1].start()
    for copy in [*give.values(), *cross.values(), *share.values(), *share_a, *share_b]:
        copy.wait_send()
    for save in saves:
        save.wait()


BEFORE = [
    "gw0", "gw1", "gw2", "gw3", "co0", "rc0", "g0", "m0", "co1", "m0", "rc1", "a0",
    "d1", "g1", "m1", "m0", "d1", "co2", "rc2", "g2", "m1", "m2", "m0", "d1",
    "co3", "m1", "rc3", "b0", "d2", "g3", "m2", "m3", "m0", "m1", "d1", "d2",
    "m0", "m2", "m3", "m0", "m1", "d1", "d2", "m2", "m1", "m3", "m0", "d1",
    "m2", "d2", "m1", "m3", "m0", "d1", "xs0", "xw0", "d2",
]
BETWEEN = {
    (0, 0, 4): ["m1", "m2"],
    (0, 0, 6): ["m3"],
    (0, 1, 2): ["m0"],
    (0, 1, 4): ["m2"],
    (0, 1, 8): ["d2"],
    (0, 1, 12): ["m1", "m3"],
    (0, 2, 0): ["m0"],
    (0, 2, 4): ["m2"],
    (0, 2, 6): ["d2", "ys0"],
    (0, 2, 14): ["m3"],
    (0, 3, 6): ["m1"],
    (0, 3, 8): ["m2"],
    (0, 3, 12): ["m3"],
    (1, 0, 0): ["m1"],
    (1, 0, 2): ["m2"],
    (1, 0, 4): ["m3"],
    (1, 1, 0): ["m2"],
    (1, 2, 0): ["m3"],
    (1, 3, 0): ["m3"],
}
MIDDLE = [
]
AFTER = [
]

def whole(cand, orbitals):
    cells = orbitals.shape[1]
    f32 = jnp.float32
    bf16 = jnp.bfloat16
    any_space = pl.BlockSpec(memory_space=pl.ANY)
    n = 2 * PIECES
    slots = []
    for rows, columns in UNIT_SHAPES:
        slots += [
            pltpu.VMEM((2, 6, rows // 8, columns), f32),
            pltpu.VMEM((2, 14, rows // 32, columns), f32),
            pltpu.VMEM((2, 2, rows // 32, columns), f32),
        ]
    return pl.pallas_call(
        whole_kernel,
        out_shape=(
            jax.ShapeDtypeStruct((ROWS, cells), bf16),
            jax.ShapeDtypeStruct((ROWS, LOCAL), f32),
            jax.ShapeDtypeStruct((ROWS, ROWS), f32),
        ),
        in_specs=[pl.BlockSpec(memory_space=pltpu.VMEM)] * 2,
        out_specs=(any_space,) * 3,
        scratch_shapes=[
            pltpu.VMEM((ROWS, cells), bf16),
            pltpu.VMEM((n, PIECE, cells), bf16),
            pltpu.VMEM((n, PIECE, cells), bf16),
            pltpu.VMEM((n, PIECE, cells), bf16),
            pltpu.VMEM((2, 256, 256), f32),
            pltpu.VMEM((2, 512, 256), f32),
            pltpu.VMEM((4, 2, B // 2, WIDE), f32),
            pltpu.VMEM((2, 256, 256), f32),
            pltpu.VMEM((2, 512, 256), f32),
            *slots,
            pltpu.VMEM((B, B), f32),
            pltpu.VMEM((BLK, BLK), f32),
            pltpu.VMEM((BLK, BLK), f32),
            pltpu.VMEM((B, B), f32),
            pltpu.VMEM((ROWS, ROWS), f32),
            pltpu.SemaphoreType.DMA((3 * n + 4,)),
            pltpu.SemaphoreType.DMA((3 * n + 4,)),
            pltpu.SemaphoreType.DMA((6, 2, COPIES)),
            pltpu.SemaphoreType.DMA((6, 2, COPIES)),
            pltpu.SemaphoreType.REGULAR((6, 2, 2)),
            pltpu.SemaphoreType.DMA((10,)),
        ],
        compiler_params=pltpu.CompilerParams(
            collective_id=0, has_side_effects=True, vmem_limit_bytes=60 << 20),
    )(cand, orbitals)


def local(orbitals, block_order):
    own_index = lax.axis_index("orb")
    local_cols = orbitals.shape[0]
    first_block = block_order[0]
    second_block = block_order[1]

    def candidate(block_index):
        piece = lax.dynamic_slice_in_dim(orbitals, block_index % BPD * B, B, 0)
        return jnp.where(block_index // BPD == own_index, piece, 0).astype(piece.dtype)

    cand = jnp.concatenate([candidate(first_block), candidate(second_block)], 0)
    panel, gram, mixing = whole(cand, orbitals)
    scale = jnp.float32(1.0 / CELLS)
    column_blocks = (own_index * local_cols + jnp.arange(local_cols, dtype=jnp.int32)) // B
    scaled = mixing * scale
    upper_first = jnp.dot(scaled[:B, :B], gram[:B], precision=lax.Precision.HIGH)
    upper_second = jnp.dot(scaled[B:], gram, precision=lax.Precision.HIGH)
    upper_second = jnp.where((column_blocks == first_block)[None, :], jnp.float32(0.0), upper_second)
    factor_rows = jnp.concatenate([upper_first, upper_second], 0)
    rows_dev = ROWS // lax.axis_size("orb")
    mixing_rows = lax.dynamic_slice_in_dim(mixing, own_index * rows_dev, rows_dev, 0)
    high = lax.reduce_precision(mixing_rows, 8, 7)
    low = (mixing_rows - high).astype(jnp.bfloat16)
    ortho = jnp.dot(high.astype(jnp.bfloat16), panel, preferred_element_type=jnp.float32) + jnp.dot(
        low, panel, preferred_element_type=jnp.float32)
    return (factor_rows, ortho)


def solution(mesh):
    return jax.shard_map(
        local,
        mesh=mesh,
        in_specs=(P("orb", "grid"), P()),
        out_specs=(P(None, "orb"), P("orb", "grid")),
        check_vma=False,
    )
```

```python
import jax
import jax.numpy as jnp
from jax import lax
from jax.experimental import pallas as pl
from jax.experimental.pallas import tpu as pltpu
from jax.sharding import PartitionSpec as P

B = 512
BPD = 4
BLK = 128
SUB = 8
HI = lax.Precision.HIGHEST


def invert_block(block_ref, out_ref, hook):
    shape = (SUB, BLK)
    lane = lax.broadcasted_iota(jnp.int32, shape, 1)
    row = lax.broadcasted_iota(jnp.int32, shape, 0)
    count = BLK // SUB
    tiles = [block_ref[SUB * i : SUB * i + SUB, :] for i in range(count)]
    for c in range(count):
        hook(c)
        low = SUB * c
        here = jnp.logical_and(lane >= low, lane < low + SUB)
        pivot = tiles[c]
        column = [jnp.broadcast_to(pivot[:, low + m : low + m + 1], shape) for m in range(SUB)]
        a = {}
        for m in range(SUB):
            for i in range(m, SUB):
                a[i, m] = jnp.broadcast_to(column[m][i : i + 1, :], shape)
        marked = jnp.where(here, (lane - low == row).astype(jnp.float32), pivot)
        y = [jnp.broadcast_to(marked[k : k + 1, :], shape) for k in range(SUB)]
        t = {}
        for m in range(SUB):
            r = lax.rsqrt(a[m, m])
            for i in range(m + 1, SUB):
                a[i, m] = a[i, m] * r
            y[m] = y[m] * r
            for k in range(m):
                t[m, k] = t[m, k] * r
            t[m, m] = r
            for j in range(m + 1, SUB):
                for i in range(j, SUB):
                    a[i, j] = a[i, j] - a[i, m] * a[j, m]
            for i in range(m + 1, SUB):
                y[i] = y[i] - a[i, m] * y[m]
                for k in range(m):
                    t[i, k] = t[i, k] - a[i, m] * t[m, k]
                t[i, m] = -(a[i, m] * r)
        tile = y[0]
        for i in range(1, SUB):
            tile = jnp.where(row == i, y[i], tile)
        out_ref[low : low + SUB, :] = jnp.where(lane < low + SUB, tile, 0.0)
        if c == count - 1:
            break
        z = []
        for k in range(SUB):
            acc = t[k, k] * y[k]
            for i in range(k + 1, SUB):
                acc = acc + t[i, k] * y[i]
            z.append(acc)
        for r in range(c + 1, count):
            terms = [jnp.broadcast_to(tiles[r][:, low + m : low + m + 1], shape) * z[m] for m in range(SUB)]
            while len(terms) > 1:
                terms = [terms[i] + terms[i + 1] for i in range(0, len(terms), 2)]
            tiles[r] = jnp.where(here, 0.0, tiles[r]) - terms[0]


ROWS = 2 * B
LOCAL = 2048
WIDE = 1024
RING = 4
PIECES = 2
PIECE = B // 2 // PIECES
CELLS = 49152
MESH = pl.DeviceIdType.MESH
UNIT_SHAPES = ((256, 256), (512, 256)) + ((256, 1024),) * 4
COPIES = 24
PEERS = [(turn, flip) for turn in range(RING) for flip in range(2)][1:]


def remote(src, dst, send, recv, axis, other):
    return pltpu.make_async_remote_copy(
        src_ref=src, dst_ref=dst, send_sem=send, recv_sem=recv, device_id={axis: other}, device_id_type=MESH)


class RingReduce:
    steps = 11

    def __init__(self, data, first, second, third, send, recv, free, p, p_next, p_prev, q, q_next, q_prev, y, device):
        y_mate = device(q, 1 - y)
        self.data, self.first, self.second, self.third, self.free = data, first, second, third, free
        self.p_ring, self.q_ring = (p_next, p_prev), (q_next, q_prev)
        size = data.shape[0]
        one, two, three = size // 4, size // 16, size // 32
        base = p * one
        low = base + q * two
        count = iter(range(COPIES))

        def make(src, dst, other):
            i = next(count)
            return remote(src, dst, send.at[i], recv.at[i], "grid", other)

        def cut(start, pos, length):
            half = length // 2
            return lambda turn, which: pl.ds(
                pl.multiple_of(start + ((pos + turn) % RING) * length + which * half, 8), half)

        def reduce_copies(rows, slots, following, previous):
            return [
                make(data.at[rows[2, 0]], slots.at[0], following),
                make(data.at[rows[2, 1]], slots.at[1], previous),
                make(data.at[rows[1, 1]], slots.at[2], following),
                make(data.at[rows[3, 0]], slots.at[3], previous),
                make(slots.at[0], slots.at[4], following),
                make(slots.at[1], slots.at[5], previous),
            ]

        def gather_copies(rows, own, following, previous):
            return [
                make(data.at[own], data.at[own], following),
                make(data.at[own], data.at[own], previous),
                make(data.at[rows[3, 0]], data.at[rows[3, 0]], following),
                make(data.at[rows[1, 1]], data.at[rows[1, 1]], previous),
            ]

        cut_p, cut_q = cut(0, p, one), cut(base, q, two)
        self.rows_p = {(t, w): cut_p(t, w) for t in range(RING) for w in range(2)}
        self.rows_q = {(t, w): cut_q(t, w) for t in range(RING) for w in range(2)}
        own_p = pl.ds(pl.multiple_of(base, 8), one)
        own_q = pl.ds(pl.multiple_of(low, 8), two)
        self.own_y = pl.ds(pl.multiple_of(low + y * three, 8), three)
        self.rest_y = pl.ds(pl.multiple_of(low + (1 - y) * three, 8), three)
        self.reduce_p = reduce_copies(self.rows_p, first, p_next, p_prev)
        self.reduce_q = reduce_copies(self.rows_q, second, q_next, q_prev)
        self.swap = make(data.at[self.rest_y], third.at[0], y_mate)
        self.share = make(data.at[self.own_y], third.at[1], y_mate)
        self.gather_q = gather_copies(self.rows_q, own_q, q_next, q_prev)
        self.gather_p = gather_copies(self.rows_p, own_p, p_next, p_prev)

    def begin(self, copies):
        for copy in copies[:4]:
            copy.start()

    def middle(self, copies, rows, slots):
        copies[0].wait_recv()
        slots[0] = slots[0] + self.data[rows[1, 0], :]
        copies[4].start()
        copies[1].wait_recv()
        slots[1] = slots[1] + self.data[rows[3, 1], :]
        copies[5].start()

    def end(self, copies, rows, slots, ring, free):
        copies[2].wait_recv()
        copies[3].wait_recv()
        copies[4].wait_recv()
        self.data[rows[0, 0], :] = self.data[rows[0, 0], :] + (slots[3] + slots[4])
        copies[5].wait_recv()
        self.data[rows[0, 1], :] = self.data[rows[0, 1], :] + (slots[2] + slots[5])
        for copy in copies:
            copy.wait_send()
        for other in ring:
            pl.semaphore_signal(free, inc=1, device_id={"grid": other}, device_id_type=MESH)

    def spread(self, copies, free):
        pl.semaphore_wait(free, 2)
        copies[0].start()
        copies[1].start()

    def forward(self, copies):
        copies[0].wait_recv()
        copies[2].start()
        copies[1].wait_recv()
        copies[3].start()

    def settle(self, copies):
        copies[2].wait_recv()
        copies[3].wait_recv()
        for copy in copies:
            copy.wait_send()

    def step(self, i):
        p, q = self.reduce_p, self.reduce_q
        if i == 0:
            self.begin(p)
        elif i == 1:
            self.middle(p, self.rows_p, self.first)
        elif i == 2:
            self.end(p, self.rows_p, self.first, self.p_ring, self.free.at[0])
            self.begin(q)
        elif i == 3:
            self.middle(q, self.rows_q, self.second)
        elif i == 4:
            self.end(q, self.rows_q, self.second, self.q_ring, self.free.at[1])
            self.swap.start()
        elif i == 5:
            self.swap.wait_recv()
            self.data[self.own_y, :] = self.data[self.own_y, :] + self.third[0]
            self.share.start()
        elif i == 6:
            self.share.wait_recv()
            self.swap.wait_send()
            self.share.wait_send()
            self.data[self.rest_y, :] = self.third[1]
            self.spread(self.gather_q, self.free.at[1])
        elif i == 7:
            self.forward(self.gather_q)
        elif i == 8:
            self.settle(self.gather_q)
            self.spread(self.gather_p, self.free.at[0])
        elif i == 9:
            self.forward(self.gather_p)
        elif i == 10:
            self.settle(self.gather_p)


class DirectReduce(RingReduce):
    steps = 7

    def __init__(self, data, first, second, third, send, recv, free, p, p_next, p_prev, q, q_next, q_prev, y, device):
        self.data, self.first, self.second, self.free = data, first, second, free
        self.p_ring = (p_next, p_prev)
        size = data.shape[0]
        one, three = size // 4, size // 32
        half = one // 2
        base = p * one
        count = iter(range(COPIES))

        def make(src, dst, other):
            i = next(count)
            return remote(src, dst, send.at[i], recv.at[i], "grid", other)

        def rows(turn, which):
            return pl.ds(pl.multiple_of(((p + turn) % RING) * one + which * half, 8), half)

        def member(turn, flip):
            return pl.ds(pl.multiple_of(base + (((q + turn) % RING) * 2 + (y + flip) % 2) * three, 8), three)

        self.rows_p = {(t, w): rows(t, w) for t in range(RING) for w in range(2)}
        self.own = member(0, 0)
        self.origin = [member(RING - turn, flip) for turn, flip in PEERS]
        own_p = pl.ds(pl.multiple_of(base, 8), one)
        others = [device((q + turn) % RING, (y + flip) % 2) for turn, flip in PEERS]
        r = self.rows_p
        self.reduce_p = [
            make(data.at[r[2, 0]], first.at[0], p_next),
            make(data.at[r[2, 1]], first.at[1], p_prev),
            make(data.at[r[1, 1]], first.at[2], p_next),
            make(data.at[r[3, 0]], first.at[3], p_prev),
            make(first.at[0], first.at[4], p_next),
            make(first.at[1], first.at[5], p_prev),
        ]
        self.scatter = [make(data.at[member(*peer)], second.at[i], others[i]) for i, peer in enumerate(PEERS)]
        self.share = [make(data.at[self.own], second.at[7 + i], others[i]) for i in range(7)]
        self.gather_p = [
            make(data.at[own_p], data.at[own_p], p_next),
            make(data.at[own_p], data.at[own_p], p_prev),
            make(data.at[r[3, 0]], data.at[r[3, 0]], p_next),
            make(data.at[r[1, 1]], data.at[r[1, 1]], p_prev),
        ]

    def step(self, i):
        p = self.reduce_p
        if i == 0:
            self.begin(p)
        elif i == 1:
            self.middle(p, self.rows_p, self.first)
        elif i == 2:
            self.end(p, self.rows_p, self.first, self.p_ring, self.free.at[0])
            for copy in self.scatter:
                copy.start()
        elif i == 3:
            total = self.data[self.own, :]
            for j, copy in enumerate(self.scatter):
                copy.wait_recv()
                total = total + self.second[j]
            self.data[self.own, :] = total
            for copy in self.share:
                copy.start()
        elif i == 4:
            for copy in self.scatter:
                copy.wait_send()
            for j, copy in enumerate(self.share):
                copy.wait_recv()
                self.data[self.origin[j], :] = self.second[7 + j]
            for copy in self.share:
                copy.wait_send()
            self.spread(self.gather_p, self.free.at[0])
        elif i == 5:
            self.forward(self.gather_p)
        elif i == 6:
            self.settle(self.gather_p)


def whole_kernel(cand_ref, orb_ref, panel_out, gram_out, mixing_out,
                 panel, merged, from_core, from_chip, tiles_a, tiles_b, main, mate_a, mate_b,
                 *rest):
    slots = [rest[3 * u : 3 * u + 3] for u in range(6)]
    work, block, inv, coupling, mixing, panel_send, panel_recv, send, recv, free, local_sem = rest[18:]
    o = lax.axis_index("orb")
    g = lax.axis_index("grid")
    core = o % 2
    mate = o + 1 - 2 * core
    across = (o + 2) % 4
    x = g // 8
    y = (g // 4) % 2
    z = g % 4
    x_next = ((x + 1) % RING) * 8 + y * 4 + z
    x_prev = ((x + 3) % RING) * 8 + y * 4 + z
    z_next = x * 8 + y * 4 + (z + 1) % RING
    z_prev = x * 8 + y * 4 + (z + 3) % RING

    def at_z(q, flip):
        return x * 8 + flip * 4 + q

    def at_x(q, flip):
        return q * 8 + flip * 4 + z

    barrier = pltpu.get_barrier_semaphore()
    near = [mate, across]
    for other in near:
        pl.semaphore_signal(barrier, inc=1, device_id={"orb": other}, device_id_type=MESH)
    far = [at_z((z + turn) % RING, (y + flip) % 2) for turn, flip in PEERS]
    far += [at_x((x + turn) % RING, (y + flip) % 2) for turn, flip in PEERS if turn]
    for other in far:
        pl.semaphore_signal(barrier, inc=1, device_id={"grid": other}, device_id_type=MESH)
    pl.semaphore_wait(barrier, len(near) + len(far))

    data = [[tiles_a.at[0], tiles_a.at[1]], [tiles_b.at[0], tiles_b.at[1]]]
    data += [[main.at[i, 0], main.at[i, 1]] for i in range(4)]
    units = []
    for u in range(6):
        kind = DirectReduce if u < 2 else RingReduce
        first, second, third = slots[u]
        units.append([
            kind(data[u][0], first.at[0], second.at[0], third.at[0], send.at[u, 0], recv.at[u, 0],
                 free.at[u, 0], x, x_next, x_prev, z, z_next, z_prev, y, at_z),
            kind(data[u][1], first.at[1], second.at[1], third.at[1], send.at[u, 1], recv.at[u, 1],
                 free.at[u, 1], z, z_next, z_prev, x, x_next, x_prev, y, at_x),
        ])
    done = [0] * 6

    def advance(u):
        for half in units[u]:
            half.step(done[u])
        done[u] += 1

    quarter = B // 2

    def part(t, which, j):
        return pl.ds(pl.multiple_of(t * B + j * quarter + which * PIECE, PIECE), PIECE)

    def orb_copy(src, dst, other, i):
        return remote(src, dst, panel_send.at[i], panel_recv.at[i], "orb", other)

    pieces = [(t, j) for t in range(2) for j in range(PIECES)]
    mine = {tj: part(tj[0], core, tj[1]) for tj in pieces}
    theirs = {tj: part(tj[0], 1 - core, tj[1]) for tj in pieces}
    n = len(pieces)
    give = {tj: orb_copy(cand_ref.at[theirs[tj]], from_core.at[i], mate, i) for i, tj in enumerate(pieces)}
    cross = {tj: orb_copy(merged.at[i], from_chip.at[i], across, n + i) for i, tj in enumerate(pieces)}
    share = {tj: orb_copy(panel.at[mine[tj]], panel.at[mine[tj]], mate, 2 * n + i) for i, tj in enumerate(pieces)}
    for tj in pieces:
        give[tj].start()

    def merge(i):
        tj = pieces[i]
        give[tj].wait_recv()
        merged[i] = cand_ref[mine[tj], :] + from_core[i]
        cross[tj].start()

    def collect(i):
        tj = pieces[i]
        cross[tj].wait_recv()
        panel[mine[tj], :] = merged[i] + from_chip[i]
        share[tj].start()

    contract = (((1,), (1,)), ((), ()))

    def product(rows, columns):
        return lax.dot_general(rows, columns, contract, preferred_element_type=jnp.float32)

    def core_rows(t):
        return panel[pl.ds(pl.multiple_of(t * B + core * quarter, quarter), quarter), :]

    def main_gram(i):
        for h in range(2):
            def column(n, carry, h=h):
                at = pl.multiple_of(n * 256, 256)
                main[i, h, :, pl.ds(at, 256)] = product(
                    panel[i * quarter : (i + 1) * quarter, :], orb_ref[pl.ds(h * WIDE + at, 256), :])
                return carry

            lax.fori_loop(0, WIDE // 256, column, 0)

    def gram_a():
        for h in range(2):
            tiles_a[h] = product(core_rows(0), panel[h * quarter : (h + 1) * quarter, :])

    save_panel = pltpu.make_async_copy(panel, panel_out, local_sem.at[0])

    def gram_b():
        for h in range(2):
            columns = panel[B + h * quarter : B + (h + 1) * quarter, :]
            tiles_b[h, :quarter, :] = product(core_rows(0), columns)
            tiles_b[h, quarter:, :] = product(core_rows(1), columns)
        save_panel.start()

    share_a = [orb_copy(tiles_a.at[h], mate_a.at[h], mate, 3 * n + h) for h in range(2)]
    share_b = [orb_copy(tiles_b.at[h], mate_b.at[h], mate, 3 * n + 2 + h) for h in range(2)]
    scale = 1.0 / CELLS
    own_rows = pl.ds(pl.multiple_of(core * quarter, quarter), quarter)
    mate_rows = pl.ds(pl.multiple_of((1 - core) * quarter, quarter), quarter)

    def start_a():
        for copy in share_a:
            copy.start()

    def start_b():
        for copy in share_b:
            copy.start()

    def load_a():
        for h in range(2):
            columns = slice(h * quarter, (h + 1) * quarter)
            work[own_rows, columns] = tiles_a[h] * scale
            share_a[h].wait_recv()
            work[mate_rows, columns] = mate_a[h] * scale

    def action(name):
        kind, i = name[:-1], int(name[-1])
        if kind == "m" or kind == "d":
            u = 1 + i if kind == "m" else i - 1
            u = u + 1 if kind == "m" else u
            now = done[u]
            done[u] += 1
            return lambda: [half.step(now) for half in units[u]]
        table = {
            "gw": merge, "co": collect, "rc": lambda j: share[pieces[j]].wait_recv(), "g": main_gram,
            "a": lambda j: gram_a(), "b": lambda j: gram_b(), "xs": lambda j: start_a(),
            "xw": lambda j: load_a(), "ys": lambda j: start_b(),
        }
        return lambda: table[kind](i)

    def perform(names):
        for name in names:
            action(name)()

    def factor(phase, hooks):
        column = lax.broadcasted_iota(jnp.int32, (BLK, B), 1)
        low = phase * B

        def step(k, carry):
            start = pl.multiple_of(k * BLK, BLK)
            here = pl.ds(start, BLK)
            block[...] = work[here, here]

            def hook(c):
                for i in range(B // BLK):
                    if (i, c) in hooks:
                        pl.when(k == i)(hooks[i, c])

            invert_block(block, inv, hook)
            t = inv[...]
            row = jnp.dot(t, work[here, :], precision=HI, preferred_element_type=jnp.float32)
            mixing[pl.ds(low + start, BLK), low : low + B] = jnp.where(column < start, row, 0.0)
            mixing[pl.ds(low + start, BLK), pl.ds(low + start, BLK)] = t
            work[here, :] = row
            work[here, here] = t

            def update(i, carry):
                rows = pl.ds(pl.multiple_of(i * BLK, BLK), BLK)
                u = work[here, rows]
                work[rows, here] = jnp.zeros((BLK, BLK), jnp.float32)
                work[rows, :] -= lax.dot_general(
                    u, work[here, :], (((0,), (0,)), ((), ())), precision=HI, preferred_element_type=jnp.float32)
                return carry

            return lax.fori_loop(k + 1, B // BLK, update, carry)

        lax.fori_loop(0, B // BLK, step, 0)

    def hooks_of(phase):
        hooks = {}
        for (at, k, c), names in BETWEEN.items():
            if at == phase:
                todo = [action(name) for name in names]
                hooks[k, c] = lambda todo=todo: [do() for do in todo] and None
        return hooks

    perform(BEFORE)
    factor(0, hooks_of(0))
    perform(MIDDLE)
    for h in range(2):
        columns = slice(h * quarter, (h + 1) * quarter)
        coupling[own_rows, columns] = tiles_b[h, :quarter, :] * scale
        work[own_rows, columns] = tiles_b[h, quarter:, :] * scale
        share_b[h].wait_recv()
        coupling[mate_rows, columns] = mate_b[h, :quarter, :] * scale
        work[mate_rows, columns] = mate_b[h, quarter:, :] * scale
    mixing[:B, B:] = jnp.zeros((B, B), jnp.float32)
    first = mixing[:B, :B]
    coupling[...] = jnp.dot(first, coupling[...], precision=HI, preferred_element_type=jnp.float32)
    turned = (((0,), (0,)), ((), ()))
    work[...] -= lax.dot_general(
        coupling[...], coupling[...], turned, precision=HI, preferred_element_type=jnp.float32)
    coupling[...] = lax.dot_general(
        coupling[...], mixing[:B, :B], turned, precision=HI, preferred_element_type=jnp.float32)
    factor(1, hooks_of(1))
    mixing[B:, :B] = -jnp.dot(mixing[B:, B:], coupling[...], precision=HI, preferred_element_type=jnp.float32)
    save_mixing = pltpu.make_async_copy(mixing, mixing_out, local_sem.at[1])
    save_mixing.start()
    saves = [save_panel, save_mixing]
    perform(AFTER)
    for i in range(4):
        assert done[2 + i] == RingReduce.steps
        for h in range(2):
            saves.append(pltpu.make_async_copy(
                main.at[i, h], gram_out.at[pl.ds(i * quarter, quarter), pl.ds(h * WIDE, WIDE)],
                local_sem.at[2 + 2 * i + h]))
            saves[-1].start()
    for copy in [*give.values(), *cross.values(), *share.values(), *share_a, *share_b]:
        copy.wait_send()
    for save in saves:
        save.wait()


BEFORE = [
    "gw0", "gw1", "gw2", "gw3", "co0", "rc0", "g0", "m0", "co1", "m0", "rc1", "a0",
    "d1", "g1", "m1", "m0", "d1", "co2", "rc2", "g2", "m1", "m2", "m0", "d1",
    "co3", "m1", "rc3", "b0", "d2", "g3", "m2", "m3", "m0", "m1", "d1", "d2",
    "m0", "m2", "m3", "m0", "m1", "d1", "d2", "m2", "m1", "m3", "m0", "d1",
    "m2", "d2", "m1", "m3", "m0", "d1", "xs0", "xw0", "d2",
]
BETWEEN = {
    (0, 0, 4): ["m1", "m2"],
    (0, 0, 6): ["m3"],
    (0, 1, 2): ["m0"],
    (0, 1, 4): ["m2"],
    (0, 1, 8): ["d2"],
    (0, 1, 12): ["m1", "m3"],
    (0, 2, 0): ["m0"],
    (0, 2, 4): ["m2"],
    (0, 2, 6): ["d2", "ys0"],
    (0, 2, 14): ["m3"],
    (0, 3, 6): ["m1"],
    (0, 3, 8): ["m2"],
    (0, 3, 12): ["m3"],
    (1, 0, 0): ["m1"],
    (1, 0, 2): ["m2"],
    (1, 0, 4): ["m3"],
    (1, 1, 0): ["m2"],
    (1, 2, 0): ["m3"],
    (1, 3, 0): ["m3"],
}
MIDDLE = [
]
AFTER = [
]

def whole(cand, orbitals):
    cells = orbitals.shape[1]
    f32 = jnp.float32
    bf16 = jnp.bfloat16
    any_space = pl.BlockSpec(memory_space=pl.ANY)
    n = 2 * PIECES
    slots = []
    for rows, columns in UNIT_SHAPES:
        slots += [
            pltpu.VMEM((2, 6, rows // 8, columns), f32),
            pltpu.VMEM((2, 14, rows // 32, columns), f32),
            pltpu.VMEM((2, 2, rows // 32, columns), f32),
        ]
    return pl.pallas_call(
        whole_kernel,
        out_shape=(
            jax.ShapeDtypeStruct((ROWS, cells), bf16),
            jax.ShapeDtypeStruct((ROWS, LOCAL), f32),
            jax.ShapeDtypeStruct((ROWS, ROWS), f32),
        ),
        in_specs=[pl.BlockSpec(memory_space=pltpu.VMEM)] * 2,
        out_specs=(any_space,) * 3,
        scratch_shapes=[
            pltpu.VMEM((ROWS, cells), bf16),
            pltpu.VMEM((n, PIECE, cells), bf16),
            pltpu.VMEM((n, PIECE, cells), bf16),
            pltpu.VMEM((n, PIECE, cells), bf16),
            pltpu.VMEM((2, 256, 256), f32),
            pltpu.VMEM((2, 512, 256), f32),
            pltpu.VMEM((4, 2, B // 2, WIDE), f32),
            pltpu.VMEM((2, 256, 256), f32),
            pltpu.VMEM((2, 512, 256), f32),
            *slots,
            pltpu.VMEM((B, B), f32),
            pltpu.VMEM((BLK, BLK), f32),
            pltpu.VMEM((BLK, BLK), f32),
            pltpu.VMEM((B, B), f32),
            pltpu.VMEM((ROWS, ROWS), f32),
            pltpu.SemaphoreType.DMA((3 * n + 4,)),
            pltpu.SemaphoreType.DMA((3 * n + 4,)),
            pltpu.SemaphoreType.DMA((6, 2, COPIES)),
            pltpu.SemaphoreType.DMA((6, 2, COPIES)),
            pltpu.SemaphoreType.REGULAR((6, 2, 2)),
            pltpu.SemaphoreType.DMA((10,)),
        ],
        compiler_params=pltpu.CompilerParams(
            collective_id=0, has_side_effects=True, vmem_limit_bytes=60 << 20),
    )(cand, orbitals)


def pick_kernel(order_ref, block_ref, out_ref):
    owner = order_ref[pl.program_id(0)] // BPD == lax.axis_index("orb")
    out_ref[...] = jnp.where(owner, block_ref[...], jnp.zeros_like(block_ref))


def pick(orbitals, block_order):
    cells = orbitals.shape[1]
    return pl.pallas_call(
        pick_kernel,
        out_shape=jax.ShapeDtypeStruct((ROWS, cells), orbitals.dtype),
        grid_spec=pltpu.PrefetchScalarGridSpec(
            num_scalar_prefetch=1,
            grid=(2,),
            in_specs=[pl.BlockSpec((B, cells), lambda i, order: (order[i] % BPD, 0))],
            out_specs=pl.BlockSpec((B, cells), lambda i, order: (i, 0)),
        ),
        compiler_params=pltpu.CompilerParams(vmem_limit_bytes=24 << 20),
    )(block_order, orbitals)


PARTS = 4


def finish_kernel(order_ref, mixing_ref, gram_ref, panel_ref, factor_ref, ortho_ref, high, low):
    n = pl.program_id(0)
    own = lax.axis_index("orb")
    quarter = ROWS // 4
    bf16 = jnp.bfloat16

    @pl.when(n == 0)
    def _():
        value = mixing_ref[...]
        high[...] = value.astype(bf16)
        low[...] = (value - high[...].astype(jnp.float32)).astype(bf16)

    def dot(a, b):
        return jnp.dot(a, b, preferred_element_type=jnp.float32)

    gram = gram_ref[...]
    gram_high = gram.astype(bf16)
    gram_low = (gram - gram_high.astype(jnp.float32)).astype(bf16)
    keep = jnp.where(own * BPD + n == order_ref[0], 0.0, 1.0 / CELLS)
    for r in range(4):
        rows = slice(r * quarter, (r + 1) * quarter)
        depth = (r + 1) * quarter
        a, b = high[rows, :depth], low[rows, :depth]
        total = dot(a, gram_high[:depth]) + (dot(a, gram_low[:depth]) + dot(b, gram_high[:depth]))
        factor_ref[rows, :] = total * (jnp.float32(1.0 / CELLS) if r < 2 else keep)
    mine = pl.ds(pl.multiple_of(own * quarter, quarter), quarter)
    panel = panel_ref[...]
    ortho_ref[...] = dot(high[mine, :], panel) + dot(low[mine, :], panel)


def finish(block_order, mixing, gram, panel):
    cells = panel.shape[1]
    f32 = jnp.float32
    return pl.pallas_call(
        finish_kernel,
        out_shape=(jax.ShapeDtypeStruct((ROWS, LOCAL), f32), jax.ShapeDtypeStruct((ROWS // 4, cells), f32)),
        grid_spec=pltpu.PrefetchScalarGridSpec(
            num_scalar_prefetch=1,
            grid=(PARTS,),
            in_specs=[
                pl.BlockSpec((ROWS, ROWS), lambda n, order: (0, 0)),
                pl.BlockSpec((ROWS, LOCAL // PARTS), lambda n, order: (0, n)),
                pl.BlockSpec((ROWS, cells // PARTS), lambda n, order: (0, n)),
            ],
            out_specs=(
                pl.BlockSpec((ROWS, LOCAL // PARTS), lambda n, order: (0, n)),
                pl.BlockSpec((ROWS // 4, cells // PARTS), lambda n, order: (0, n)),
            ),
            scratch_shapes=[pltpu.VMEM((ROWS, ROWS), jnp.bfloat16)] * 2,
        ),
        compiler_params=pltpu.CompilerParams(vmem_limit_bytes=48 << 20),
    )(block_order, mixing, gram, panel)


def local(orbitals, block_order):
    panel, gram, mixing = whole(pick(orbitals, block_order), orbitals)
    return finish(block_order, mixing, gram, panel)


def solution(mesh):
    return jax.shard_map(
        local,
        mesh=mesh,
        in_specs=(P("orb", "grid"), P()),
        out_specs=(P(None, "orb"), P("orb", "grid")),
        check_vma=False,
    )
```

```python
import jax
import jax.numpy as jnp
from jax import lax
from jax.experimental import pallas as pl
from jax.experimental.pallas import tpu as pltpu
from jax.sharding import PartitionSpec as P

B = 512
BPD = 4
BLK = 128
SUB = 8
HI = lax.Precision.HIGHEST


def invert_block(block_ref, out_ref, hook):
    shape = (SUB, BLK)
    lane = lax.broadcasted_iota(jnp.int32, shape, 1)
    row = lax.broadcasted_iota(jnp.int32, shape, 0)
    count = BLK // SUB
    tiles = [block_ref[SUB * i : SUB * i + SUB, :] for i in range(count)]
    for c in range(count):
        hook(c)
        low = SUB * c
        here = jnp.logical_and(lane >= low, lane < low + SUB)
        pivot = tiles[c]
        column = [jnp.broadcast_to(pivot[:, low + m : low + m + 1], shape) for m in range(SUB)]
        a = {}
        for m in range(SUB):
            for i in range(m, SUB):
                a[i, m] = jnp.broadcast_to(column[m][i : i + 1, :], shape)
        marked = jnp.where(here, (lane - low == row).astype(jnp.float32), pivot)
        y = [jnp.broadcast_to(marked[k : k + 1, :], shape) for k in range(SUB)]
        t = {}
        for m in range(SUB):
            r = lax.rsqrt(a[m, m])
            for i in range(m + 1, SUB):
                a[i, m] = a[i, m] * r
            y[m] = y[m] * r
            for k in range(m):
                t[m, k] = t[m, k] * r
            t[m, m] = r
            for j in range(m + 1, SUB):
                for i in range(j, SUB):
                    a[i, j] = a[i, j] - a[i, m] * a[j, m]
            for i in range(m + 1, SUB):
                y[i] = y[i] - a[i, m] * y[m]
                for k in range(m):
                    t[i, k] = t[i, k] - a[i, m] * t[m, k]
                t[i, m] = -(a[i, m] * r)
        tile = y[0]
        for i in range(1, SUB):
            tile = jnp.where(row == i, y[i], tile)
        out_ref[low : low + SUB, :] = jnp.where(lane < low + SUB, tile, 0.0)
        if c == count - 1:
            break
        z = []
        for k in range(SUB):
            acc = t[k, k] * y[k]
            for i in range(k + 1, SUB):
                acc = acc + t[i, k] * y[i]
            z.append(acc)
        for r in range(c + 1, count):
            terms = [jnp.broadcast_to(tiles[r][:, low + m : low + m + 1], shape) * z[m] for m in range(SUB)]
            while len(terms) > 1:
                terms = [terms[i] + terms[i + 1] for i in range(0, len(terms), 2)]
            tiles[r] = jnp.where(here, 0.0, tiles[r]) - terms[0]


ROWS = 2 * B
LOCAL = 2048
WIDE = 1024
RING = 4
PIECES = 2
PIECE = B // 2 // PIECES
CELLS = 49152
MESH = pl.DeviceIdType.MESH
UNIT_SHAPES = ((256, 256), (512, 256)) + ((256, 1024),) * 4
COPIES = 24
PEERS = [(turn, flip) for turn in range(RING) for flip in range(2)][1:]


def remote(src, dst, send, recv, axis, other):
    return pltpu.make_async_remote_copy(
        src_ref=src, dst_ref=dst, send_sem=send, recv_sem=recv, device_id={axis: other}, device_id_type=MESH)


class RingReduce:
    steps = 11

    def __init__(self, data, first, second, third, send, recv, free, p, p_next, p_prev, q, q_next, q_prev, y, device):
        y_mate = device(q, 1 - y)
        self.data, self.first, self.second, self.third, self.free = data, first, second, third, free
        self.p_ring, self.q_ring = (p_next, p_prev), (q_next, q_prev)
        size = data.shape[0]
        one, two, three = size // 4, size // 16, size // 32
        base = p * one
        low = base + q * two
        count = iter(range(COPIES))

        def make(src, dst, other):
            i = next(count)
            return remote(src, dst, send.at[i], recv.at[i], "grid", other)

        def cut(start, pos, length):
            half = length // 2
            return lambda turn, which: pl.ds(
                pl.multiple_of(start + ((pos + turn) % RING) * length + which * half, 8), half)

        def reduce_copies(rows, slots, following, previous):
            return [
                make(data.at[rows[2, 0]], slots.at[0], following),
                make(data.at[rows[2, 1]], slots.at[1], previous),
                make(data.at[rows[1, 1]], slots.at[2], following),
                make(data.at[rows[3, 0]], slots.at[3], previous),
                make(slots.at[0], slots.at[4], following),
                make(slots.at[1], slots.at[5], previous),
            ]

        def gather_copies(rows, own, following, previous):
            return [
                make(data.at[own], data.at[own], following),
                make(data.at[own], data.at[own], previous),
                make(data.at[rows[3, 0]], data.at[rows[3, 0]], following),
                make(data.at[rows[1, 1]], data.at[rows[1, 1]], previous),
            ]

        cut_p, cut_q = cut(0, p, one), cut(base, q, two)
        self.rows_p = {(t, w): cut_p(t, w) for t in range(RING) for w in range(2)}
        self.rows_q = {(t, w): cut_q(t, w) for t in range(RING) for w in range(2)}
        own_p = pl.ds(pl.multiple_of(base, 8), one)
        own_q = pl.ds(pl.multiple_of(low, 8), two)
        self.own_y = pl.ds(pl.multiple_of(low + y * three, 8), three)
        self.rest_y = pl.ds(pl.multiple_of(low + (1 - y) * three, 8), three)
        self.reduce_p = reduce_copies(self.rows_p, first, p_next, p_prev)
        self.reduce_q = reduce_copies(self.rows_q, second, q_next, q_prev)
        self.swap = make(data.at[self.rest_y], third.at[0], y_mate)
        self.share = make(data.at[self.own_y], third.at[1], y_mate)
        self.gather_q = gather_copies(self.rows_q, own_q, q_next, q_prev)
        self.gather_p = gather_copies(self.rows_p, own_p, p_next, p_prev)

    def begin(self, copies):
        for copy in copies[:4]:
            copy.start()

    def middle(self, copies, rows, slots):
        copies[0].wait_recv()
        slots[0] = slots[0] + self.data[rows[1, 0], :]
        copies[4].start()
        copies[1].wait_recv()
        slots[1] = slots[1] + self.data[rows[3, 1], :]
        copies[5].start()

    def end(self, copies, rows, slots, ring, free):
        copies[2].wait_recv()
        copies[3].wait_recv()
        copies[4].wait_recv()
        self.data[rows[0, 0], :] = self.data[rows[0, 0], :] + (slots[3] + slots[4])
        copies[5].wait_recv()
        self.data[rows[0, 1], :] = self.data[rows[0, 1], :] + (slots[2] + slots[5])
        for copy in copies:
            copy.wait_send()
        for other in ring:
            pl.semaphore_signal(free, inc=1, device_id={"grid": other}, device_id_type=MESH)

    def spread(self, copies, free):
        pl.semaphore_wait(free, 2)
        copies[0].start()
        copies[1].start()

    def forward(self, copies):
        copies[0].wait_recv()
        copies[2].start()
        copies[1].wait_recv()
        copies[3].start()

    def settle(self, copies):
        copies[2].wait_recv()
        copies[3].wait_recv()
        for copy in copies:
            copy.wait_send()

    def step(self, i):
        p, q = self.reduce_p, self.reduce_q
        if i == 0:
            self.begin(p)
        elif i == 1:
            self.middle(p, self.rows_p, self.first)
        elif i == 2:
            self.end(p, self.rows_p, self.first, self.p_ring, self.free.at[0])
            self.begin(q)
        elif i == 3:
            self.middle(q, self.rows_q, self.second)
        elif i == 4:
            self.end(q, self.rows_q, self.second, self.q_ring, self.free.at[1])
            self.swap.start()
        elif i == 5:
            self.swap.wait_recv()
            self.data[self.own_y, :] = self.data[self.own_y, :] + self.third[0]
            self.share.start()
        elif i == 6:
            self.share.wait_recv()
            self.swap.wait_send()
            self.share.wait_send()
            self.data[self.rest_y, :] = self.third[1]
            self.spread(self.gather_q, self.free.at[1])
        elif i == 7:
            self.forward(self.gather_q)
        elif i == 8:
            self.settle(self.gather_q)
            self.spread(self.gather_p, self.free.at[0])
        elif i == 9:
            self.forward(self.gather_p)
        elif i == 10:
            self.settle(self.gather_p)


class DirectReduce(RingReduce):
    steps = 7

    def __init__(self, data, first, second, third, send, recv, free, p, p_next, p_prev, q, q_next, q_prev, y, device):
        self.data, self.first, self.second, self.free = data, first, second, free
        self.p_ring = (p_next, p_prev)
        size = data.shape[0]
        one, three = size // 4, size // 32
        half = one // 2
        base = p * one
        count = iter(range(COPIES))

        def make(src, dst, other):
            i = next(count)
            return remote(src, dst, send.at[i], recv.at[i], "grid", other)

        def rows(turn, which):
            return pl.ds(pl.multiple_of(((p + turn) % RING) * one + which * half, 8), half)

        def member(turn, flip):
            return pl.ds(pl.multiple_of(base + (((q + turn) % RING) * 2 + (y + flip) % 2) * three, 8), three)

        self.rows_p = {(t, w): rows(t, w) for t in range(RING) for w in range(2)}
        self.own = member(0, 0)
        self.origin = [member(RING - turn, flip) for turn, flip in PEERS]
        own_p = pl.ds(pl.multiple_of(base, 8), one)
        others = [device((q + turn) % RING, (y + flip) % 2) for turn, flip in PEERS]
        r = self.rows_p
        self.reduce_p = [
            make(data.at[r[2, 0]], first.at[0], p_next),
            make(data.at[r[2, 1]], first.at[1], p_prev),
            make(data.at[r[1, 1]], first.at[2], p_next),
            make(data.at[r[3, 0]], first.at[3], p_prev),
            make(first.at[0], first.at[4], p_next),
            make(first.at[1], first.at[5], p_prev),
        ]
        self.scatter = [make(data.at[member(*peer)], second.at[i], others[i]) for i, peer in enumerate(PEERS)]
        self.share = [make(data.at[self.own], second.at[7 + i], others[i]) for i in range(7)]
        self.gather_p = [
            make(data.at[own_p], data.at[own_p], p_next),
            make(data.at[own_p], data.at[own_p], p_prev),
            make(data.at[r[3, 0]], data.at[r[3, 0]], p_next),
            make(data.at[r[1, 1]], data.at[r[1, 1]], p_prev),
        ]

    def step(self, i):
        p = self.reduce_p
        if i == 0:
            self.begin(p)
        elif i == 1:
            self.middle(p, self.rows_p, self.first)
        elif i == 2:
            self.end(p, self.rows_p, self.first, self.p_ring, self.free.at[0])
            for copy in self.scatter:
                copy.start()
        elif i == 3:
            total = self.data[self.own, :]
            for j, copy in enumerate(self.scatter):
                copy.wait_recv()
                total = total + self.second[j]
            self.data[self.own, :] = total
            for copy in self.share:
                copy.start()
        elif i == 4:
            for copy in self.scatter:
                copy.wait_send()
            for j, copy in enumerate(self.share):
                copy.wait_recv()
                self.data[self.origin[j], :] = self.second[7 + j]
            for copy in self.share:
                copy.wait_send()
            self.spread(self.gather_p, self.free.at[0])
        elif i == 5:
            self.forward(self.gather_p)
        elif i == 6:
            self.settle(self.gather_p)


def whole_kernel(cand_ref, orb_ref, panel_out, gram_out, mixing_out,
                 panel, merged, from_core, from_chip, tiles_a, tiles_b, main, mate_a, mate_b,
                 *rest):
    slots = [rest[3 * u : 3 * u + 3] for u in range(6)]
    work, block, inv, coupling, mixing, orbitals, panel_send, panel_recv, send, recv, free, local_sem = rest[18:]
    load = pltpu.make_async_copy(orb_ref, orbitals, local_sem.at[10])
    load.start()
    o = lax.axis_index("orb")
    g = lax.axis_index("grid")
    core = o % 2
    mate = o + 1 - 2 * core
    across = (o + 2) % 4
    x = g // 8
    y = (g // 4) % 2
    z = g % 4
    x_next = ((x + 1) % RING) * 8 + y * 4 + z
    x_prev = ((x + 3) % RING) * 8 + y * 4 + z
    z_next = x * 8 + y * 4 + (z + 1) % RING
    z_prev = x * 8 + y * 4 + (z + 3) % RING

    def at_z(q, flip):
        return x * 8 + flip * 4 + q

    def at_x(q, flip):
        return q * 8 + flip * 4 + z

    barrier = pltpu.get_barrier_semaphore()
    near = [mate, across]
    for other in near:
        pl.semaphore_signal(barrier, inc=1, device_id={"orb": other}, device_id_type=MESH)
    far = [at_z((z + turn) % RING, (y + flip) % 2) for turn, flip in PEERS]
    far += [at_x((x + turn) % RING, (y + flip) % 2) for turn, flip in PEERS if turn]
    for other in far:
        pl.semaphore_signal(barrier, inc=1, device_id={"grid": other}, device_id_type=MESH)
    pl.semaphore_wait(barrier, len(near) + len(far))

    data = [[tiles_a.at[0], tiles_a.at[1]], [tiles_b.at[0], tiles_b.at[1]]]
    data += [[main.at[i, 0], main.at[i, 1]] for i in range(4)]
    units = []
    for u in range(6):
        kind = DirectReduce if u < 2 else RingReduce
        first, second, third = slots[u]
        units.append([
            kind(data[u][0], first.at[0], second.at[0], third.at[0], send.at[u, 0], recv.at[u, 0],
                 free.at[u, 0], x, x_next, x_prev, z, z_next, z_prev, y, at_z),
            kind(data[u][1], first.at[1], second.at[1], third.at[1], send.at[u, 1], recv.at[u, 1],
                 free.at[u, 1], z, z_next, z_prev, x, x_next, x_prev, y, at_x),
        ])
    done = [0] * 6

    def advance(u):
        for half in units[u]:
            half.step(done[u])
        done[u] += 1

    quarter = B // 2

    def part(t, which, j):
        return pl.ds(pl.multiple_of(t * B + j * quarter + which * PIECE, PIECE), PIECE)

    def orb_copy(src, dst, other, i):
        return remote(src, dst, panel_send.at[i], panel_recv.at[i], "orb", other)

    pieces = [(t, j) for t in range(2) for j in range(PIECES)]
    mine = {tj: part(tj[0], core, tj[1]) for tj in pieces}
    theirs = {tj: part(tj[0], 1 - core, tj[1]) for tj in pieces}
    n = len(pieces)
    give = {tj: orb_copy(cand_ref.at[theirs[tj]], from_core.at[i], mate, i) for i, tj in enumerate(pieces)}
    cross = {tj: orb_copy(merged.at[i], from_chip.at[i], across, n + i) for i, tj in enumerate(pieces)}
    share = {tj: orb_copy(panel.at[mine[tj]], panel.at[mine[tj]], mate, 2 * n + i) for i, tj in enumerate(pieces)}
    for tj in pieces:
        give[tj].start()

    def merge(i):
        tj = pieces[i]
        give[tj].wait_recv()
        merged[i] = cand_ref[mine[tj], :] + from_core[i]
        cross[tj].start()

    def collect(i):
        tj = pieces[i]
        cross[tj].wait_recv()
        panel[mine[tj], :] = merged[i] + from_chip[i]
        share[tj].start()

    contract = (((1,), (1,)), ((), ()))

    def product(rows, columns):
        return lax.dot_general(rows, columns, contract, preferred_element_type=jnp.float32)

    def core_rows(t):
        return panel[pl.ds(pl.multiple_of(t * B + core * quarter, quarter), quarter), :]

    def main_gram(i):
        if i == 0:
            load.wait()
        for h in range(2):
            def column(n, carry, h=h):
                at = pl.multiple_of(n * 256, 256)
                main[i, h, :, pl.ds(at, 256)] = product(
                    panel[i * quarter : (i + 1) * quarter, :], orbitals[pl.ds(h * WIDE + at, 256), :])
                return carry

            lax.fori_loop(0, WIDE // 256, column, 0)

    def gram_a():
        for h in range(2):
            tiles_a[h] = product(core_rows(0), panel[h * quarter : (h + 1) * quarter, :])

    save_panel = pltpu.make_async_copy(panel, panel_out, local_sem.at[0])

    def gram_b():
        for h in range(2):
            columns = panel[B + h * quarter : B + (h + 1) * quarter, :]
            tiles_b[h, :quarter, :] = product(core_rows(0), columns)
            tiles_b[h, quarter:, :] = product(core_rows(1), columns)
        save_panel.start()

    share_a = [orb_copy(tiles_a.at[h], mate_a.at[h], mate, 3 * n + h) for h in range(2)]
    share_b = [orb_copy(tiles_b.at[h], mate_b.at[h], mate, 3 * n + 2 + h) for h in range(2)]
    scale = 1.0 / CELLS
    own_rows = pl.ds(pl.multiple_of(core * quarter, quarter), quarter)
    mate_rows = pl.ds(pl.multiple_of((1 - core) * quarter, quarter), quarter)

    def start_a():
        for copy in share_a:
            copy.start()

    def start_b():
        for copy in share_b:
            copy.start()

    def load_a():
        for h in range(2):
            columns = slice(h * quarter, (h + 1) * quarter)
            work[own_rows, columns] = tiles_a[h] * scale
            share_a[h].wait_recv()
            work[mate_rows, columns] = mate_a[h] * scale

    def action(name):
        kind, i = name[:-1], int(name[-1])
        if kind == "m" or kind == "d":
            u = 1 + i if kind == "m" else i - 1
            u = u + 1 if kind == "m" else u
            now = done[u]
            done[u] += 1
            return lambda: [half.step(now) for half in units[u]]
        table = {
            "gw": merge, "co": collect, "rc": lambda j: share[pieces[j]].wait_recv(), "g": main_gram,
            "a": lambda j: gram_a(), "b": lambda j: gram_b(), "xs": lambda j: start_a(),
            "xw": lambda j: load_a(), "ys": lambda j: start_b(),
        }
        return lambda: table[kind](i)

    def perform(names):
        for name in names:
            action(name)()

    def factor(phase, hooks):
        column = lax.broadcasted_iota(jnp.int32, (BLK, B), 1)
        low = phase * B

        def step(k, carry):
            start = pl.multiple_of(k * BLK, BLK)
            here = pl.ds(start, BLK)
            block[...] = work[here, here]

            def hook(c):
                for i in range(B // BLK):
                    if (i, c) in hooks:
                        pl.when(k == i)(hooks[i, c])

            invert_block(block, inv, hook)
            t = inv[...]
            row = jnp.dot(t, work[here, :], precision=HI, preferred_element_type=jnp.float32)
            mixing[pl.ds(low + start, BLK), low : low + B] = jnp.where(column < start, row, 0.0)
            mixing[pl.ds(low + start, BLK), pl.ds(low + start, BLK)] = t
            work[here, :] = row
            work[here, here] = t

            def update(i, carry):
                rows = pl.ds(pl.multiple_of(i * BLK, BLK), BLK)
                u = work[here, rows]
                work[rows, here] = jnp.zeros((BLK, BLK), jnp.float32)
                work[rows, :] -= lax.dot_general(
                    u, work[here, :], (((0,), (0,)), ((), ())), precision=HI, preferred_element_type=jnp.float32)
                return carry

            return lax.fori_loop(k + 1, B // BLK, update, carry)

        lax.fori_loop(0, B // BLK, step, 0)

    def hooks_of(phase):
        hooks = {}
        for (at, k, c), names in BETWEEN.items():
            if at == phase:
                todo = [action(name) for name in names]
                hooks[k, c] = lambda todo=todo: [do() for do in todo] and None
        return hooks

    perform(BEFORE)
    factor(0, hooks_of(0))
    perform(MIDDLE)
    for h in range(2):
        columns = slice(h * quarter, (h + 1) * quarter)
        coupling[own_rows, columns] = tiles_b[h, :quarter, :] * scale
        work[own_rows, columns] = tiles_b[h, quarter:, :] * scale
        share_b[h].wait_recv()
        coupling[mate_rows, columns] = mate_b[h, :quarter, :] * scale
        work[mate_rows, columns] = mate_b[h, quarter:, :] * scale
    mixing[:B, B:] = jnp.zeros((B, B), jnp.float32)
    first = mixing[:B, :B]
    coupling[...] = jnp.dot(first, coupling[...], precision=HI, preferred_element_type=jnp.float32)
    turned = (((0,), (0,)), ((), ()))
    work[...] -= lax.dot_general(
        coupling[...], coupling[...], turned, precision=HI, preferred_element_type=jnp.float32)
    coupling[...] = lax.dot_general(
        coupling[...], mixing[:B, :B], turned, precision=HI, preferred_element_type=jnp.float32)
    factor(1, hooks_of(1))
    mixing[B:, :B] = -jnp.dot(mixing[B:, B:], coupling[...], precision=HI, preferred_element_type=jnp.float32)
    save_mixing = pltpu.make_async_copy(mixing, mixing_out, local_sem.at[1])
    save_mixing.start()
    saves = [save_panel, save_mixing]
    perform(AFTER)
    for i in range(4):
        assert done[2 + i] == RingReduce.steps
        for h in range(2):
            saves.append(pltpu.make_async_copy(
                main.at[i, h], gram_out.at[pl.ds(i * quarter, quarter), pl.ds(h * WIDE, WIDE)],
                local_sem.at[2 + 2 * i + h]))
            saves[-1].start()
    for copy in [*give.values(), *cross.values(), *share.values(), *share_a, *share_b]:
        copy.wait_send()
    for save in saves:
        save.wait()


BEFORE = [
    "gw0", "gw1", "gw2", "gw3", "co0", "rc0", "g0", "m0", "co1", "m0", "rc1", "a0",
    "d1", "g1", "m1", "m0", "d1", "co2", "rc2", "g2", "m1", "m2", "m0", "d1",
    "co3", "m1", "rc3", "b0", "d2", "g3", "m2", "m3", "m0", "m1", "d1", "d2",
    "m0", "m2", "m3", "m0", "m1", "d1", "d2", "m2", "m1", "m3", "m0", "d1",
    "m2", "d2", "m1", "m3", "m0", "d1", "xs0", "xw0", "d2",
]
BETWEEN = {
    (0, 0, 10): ["m2", "m1"],
    (0, 0, 12): ["m3"],
    (0, 1, 8): ["d2", "m0"],
    (0, 2, 0): ["d2", "ys0", "m1", "m2"],
    (0, 2, 4): ["m3"],
    (0, 3, 0): ["m0"],
    (0, 3, 12): ["m3"],
    (0, 3, 14): ["m1"],
    (1, 0, 0): ["m3", "m1"],
    (1, 0, 2): ["m2"],
    (1, 1, 0): ["m3"],
    (1, 2, 0): ["m2"],
    (1, 2, 14): ["m3"],
    (1, 3, 6): ["m2"],
}
MIDDLE = [
    "m2",
]
AFTER = [
    "m3",
]

def whole(cand, orbitals):
    cells = orbitals.shape[1]
    f32 = jnp.float32
    bf16 = jnp.bfloat16
    any_space = pl.BlockSpec(memory_space=pl.ANY)
    n = 2 * PIECES
    slots = []
    for rows, columns in UNIT_SHAPES:
        slots += [
            pltpu.VMEM((2, 6, rows // 8, columns), f32),
            pltpu.VMEM((2, 14, rows // 32, columns), f32),
            pltpu.VMEM((2, 2, rows // 32, columns), f32),
        ]
    return pl.pallas_call(
        whole_kernel,
        out_shape=(
            jax.ShapeDtypeStruct((ROWS, cells), bf16),
            jax.ShapeDtypeStruct((ROWS, LOCAL), f32),
            jax.ShapeDtypeStruct((ROWS, ROWS), f32),
        ),
        in_specs=[pl.BlockSpec(memory_space=pltpu.VMEM), any_space],
        out_specs=(any_space,) * 3,
        scratch_shapes=[
            pltpu.VMEM((ROWS, cells), bf16),
            pltpu.VMEM((n, PIECE, cells), bf16),
            pltpu.VMEM((n, PIECE, cells), bf16),
            pltpu.VMEM((n, PIECE, cells), bf16),
            pltpu.VMEM((2, 256, 256), f32),
            pltpu.VMEM((2, 512, 256), f32),
            pltpu.VMEM((4, 2, B // 2, WIDE), f32),
            pltpu.VMEM((2, 256, 256), f32),
            pltpu.VMEM((2, 512, 256), f32),
            *slots,
            pltpu.VMEM((B, B), f32),
            pltpu.VMEM((BLK, BLK), f32),
            pltpu.VMEM((BLK, BLK), f32),
            pltpu.VMEM((B, B), f32),
            pltpu.VMEM((ROWS, ROWS), f32),
            pltpu.VMEM((LOCAL, cells), bf16),
            pltpu.SemaphoreType.DMA((3 * n + 4,)),
            pltpu.SemaphoreType.DMA((3 * n + 4,)),
            pltpu.SemaphoreType.DMA((6, 2, COPIES)),
            pltpu.SemaphoreType.DMA((6, 2, COPIES)),
            pltpu.SemaphoreType.REGULAR((6, 2, 2)),
            pltpu.SemaphoreType.DMA((11,)),
        ],
        compiler_params=pltpu.CompilerParams(
            collective_id=0, has_side_effects=True, vmem_limit_bytes=60 << 20),
    )(cand, orbitals)


def pick_kernel(order_ref, block_ref, out_ref):
    owner = order_ref[pl.program_id(0)] // BPD == lax.axis_index("orb")
    out_ref[...] = jnp.where(owner, block_ref[...], jnp.zeros_like(block_ref))


def pick(orbitals, block_order):
    cells = orbitals.shape[1]
    return pl.pallas_call(
        pick_kernel,
        out_shape=jax.ShapeDtypeStruct((ROWS, cells), orbitals.dtype),
        grid_spec=pltpu.PrefetchScalarGridSpec(
            num_scalar_prefetch=1,
            grid=(2,),
            in_specs=[pl.BlockSpec((B, cells), lambda i, order: (order[i] % BPD, 0))],
            out_specs=pl.BlockSpec((B, cells), lambda i, order: (i, 0)),
        ),
        compiler_params=pltpu.CompilerParams(vmem_limit_bytes=60 << 20),
    )(block_order, orbitals)


PARTS = 4


def finish_kernel(order_ref, mixing_ref, gram_ref, panel_ref, factor_ref, ortho_ref, left, right):
    n = pl.program_id(0)
    own = lax.axis_index("orb")
    quarter = ROWS // 4
    bf16 = jnp.bfloat16

    @pl.when(n == 0)
    def _():
        for k in range(4):
            value = mixing_ref[:, k * quarter : (k + 1) * quarter]
            high = value.astype(bf16)
            left[:, 3 * k * quarter : (3 * k + 1) * quarter] = high
            left[:, (3 * k + 1) * quarter : (3 * k + 2) * quarter] = high
            left[:, (3 * k + 2) * quarter : (3 * k + 3) * quarter] = (value - high.astype(jnp.float32)).astype(bf16)

    def dot(a, b):
        return jnp.dot(a, b, preferred_element_type=jnp.float32)

    for k in range(4):
        value = gram_ref[k * quarter : (k + 1) * quarter, :]
        high = value.astype(bf16)
        right[3 * k * quarter : (3 * k + 1) * quarter, :] = high
        right[(3 * k + 1) * quarter : (3 * k + 2) * quarter, :] = (value - high.astype(jnp.float32)).astype(bf16)
        right[(3 * k + 2) * quarter : (3 * k + 3) * quarter, :] = high
    keep = jnp.where(own * BPD + n == order_ref[0], 0.0, 1.0 / CELLS)
    for r in range(4):
        rows = slice(r * quarter, (r + 1) * quarter)
        depth = 3 * (r + 1) * quarter
        total = dot(left[rows, :depth], right[:depth, :])
        factor_ref[rows, :] = total * (jnp.float32(1.0 / CELLS) if r < 2 else keep)
    mine = pl.ds(pl.multiple_of(own * quarter, quarter), quarter)
    total = jnp.zeros(ortho_ref.shape, jnp.float32)
    for k in range(4):
        panel = panel_ref[k * quarter : (k + 1) * quarter, :]
        for part in (0, 2):
            total += dot(left[mine, (3 * k + part) * quarter : (3 * k + part + 1) * quarter], panel)
    ortho_ref[...] = total


def finish(block_order, mixing, gram, panel):
    cells = panel.shape[1]
    f32 = jnp.float32
    return pl.pallas_call(
        finish_kernel,
        out_shape=(jax.ShapeDtypeStruct((ROWS, LOCAL), f32), jax.ShapeDtypeStruct((ROWS // 4, cells), f32)),
        grid_spec=pltpu.PrefetchScalarGridSpec(
            num_scalar_prefetch=1,
            grid=(PARTS,),
            in_specs=[
                pl.BlockSpec((ROWS, ROWS), lambda n, order: (0, 0)),
                pl.BlockSpec((ROWS, LOCAL // PARTS), lambda n, order: (0, n)),
                pl.BlockSpec((ROWS, cells // PARTS), lambda n, order: (0, n)),
            ],
            out_specs=(
                pl.BlockSpec((ROWS, LOCAL // PARTS), lambda n, order: (0, n)),
                pl.BlockSpec((ROWS // 4, cells // PARTS), lambda n, order: (0, n)),
            ),
            scratch_shapes=[
                pltpu.VMEM((ROWS, 3 * ROWS), jnp.bfloat16),
                pltpu.VMEM((3 * ROWS, LOCAL // PARTS), jnp.bfloat16),
            ],
        ),
        compiler_params=pltpu.CompilerParams(vmem_limit_bytes=60 << 20),
    )(block_order, mixing, gram, panel)


def local(orbitals, block_order):
    panel, gram, mixing = whole(pick(orbitals, block_order), orbitals)
    return finish(block_order, mixing, gram, panel)


def solution(mesh):
    return jax.shard_map(
        local,
        mesh=mesh,
        in_specs=(P("orb", "grid"), P()),
        out_specs=(P(None, "orb"), P("orb", "grid")),
        check_vma=False,
    )
```

```python
import jax
import jax.numpy as jnp
from jax import lax
from jax.experimental import pallas as pl
from jax.experimental.pallas import tpu as pltpu
from jax.sharding import PartitionSpec as P

B = 512
BPD = 4
BLK = 128
SUB = 8
HI = lax.Precision.HIGHEST


def invert_block(block_ref, out_ref, hook):
    shape = (SUB, BLK)
    lane = lax.broadcasted_iota(jnp.int32, shape, 1)
    row = lax.broadcasted_iota(jnp.int32, shape, 0)
    count = BLK // SUB
    tiles = [block_ref[SUB * i : SUB * i + SUB, :] for i in range(count)]
    for c in range(count):
        hook(c)
        low = SUB * c
        here = jnp.logical_and(lane >= low, lane < low + SUB)
        pivot = tiles[c]
        column = [jnp.broadcast_to(pivot[:, low + m : low + m + 1], shape) for m in range(SUB)]
        a = {}
        for m in range(SUB):
            for i in range(m, SUB):
                a[i, m] = jnp.broadcast_to(column[m][i : i + 1, :], shape)
        marked = jnp.where(here, (lane - low == row).astype(jnp.float32), pivot)
        y = [jnp.broadcast_to(marked[k : k + 1, :], shape) for k in range(SUB)]
        t = {}
        for m in range(SUB):
            r = lax.rsqrt(a[m, m])
            for i in range(m + 1, SUB):
                a[i, m] = a[i, m] * r
            y[m] = y[m] * r
            for k in range(m):
                t[m, k] = t[m, k] * r
            t[m, m] = r
            for j in range(m + 1, SUB):
                for i in range(j, SUB):
                    a[i, j] = a[i, j] - a[i, m] * a[j, m]
            for i in range(m + 1, SUB):
                y[i] = y[i] - a[i, m] * y[m]
                for k in range(m):
                    t[i, k] = t[i, k] - a[i, m] * t[m, k]
                t[i, m] = -(a[i, m] * r)
        tile = y[0]
        for i in range(1, SUB):
            tile = jnp.where(row == i, y[i], tile)
        out_ref[low : low + SUB, :] = jnp.where(lane < low + SUB, tile, 0.0)
        if c == count - 1:
            break
        z = []
        for k in range(SUB):
            acc = t[k, k] * y[k]
            for i in range(k + 1, SUB):
                acc = acc + t[i, k] * y[i]
            z.append(acc)
        for r in range(c + 1, count):
            terms = [jnp.broadcast_to(tiles[r][:, low + m : low + m + 1], shape) * z[m] for m in range(SUB)]
            while len(terms) > 1:
                terms = [terms[i] + terms[i + 1] for i in range(0, len(terms), 2)]
            tiles[r] = jnp.where(here, 0.0, tiles[r]) - terms[0]


ROWS = 2 * B
LOCAL = 2048
WIDE = 1024
RING = 4
PIECES = 2
PIECE = B // 2 // PIECES
CELLS = 49152
MESH = pl.DeviceIdType.MESH
UNIT_SHAPES = ((256, 256), (512, 256)) + ((256, 1024),) * 4
COPIES = 24
PEERS = [(turn, flip) for turn in range(RING) for flip in range(2)][1:]


def remote(src, dst, send, recv, axis, other):
    return pltpu.make_async_remote_copy(
        src_ref=src, dst_ref=dst, send_sem=send, recv_sem=recv, device_id={axis: other}, device_id_type=MESH)


class RingReduce:
    steps = 11

    def __init__(self, data, first, second, third, send, recv, free, p, p_next, p_prev, q, q_next, q_prev, y, device):
        y_mate = device(q, 1 - y)
        self.data, self.first, self.second, self.third, self.free = data, first, second, third, free
        self.p_ring, self.q_ring = (p_next, p_prev), (q_next, q_prev)
        size = data.shape[0]
        one, two, three = size // 4, size // 16, size // 32
        base = p * one
        low = base + q * two
        count = iter(range(COPIES))

        def make(src, dst, other):
            i = next(count)
            return remote(src, dst, send.at[i], recv.at[i], "grid", other)

        def cut(start, pos, length):
            half = length // 2
            return lambda turn, which: pl.ds(
                pl.multiple_of(start + ((pos + turn) % RING) * length + which * half, 8), half)

        def reduce_copies(rows, slots, following, previous):
            return [
                make(data.at[rows[2, 0]], slots.at[0], following),
                make(data.at[rows[2, 1]], slots.at[1], previous),
                make(data.at[rows[1, 1]], slots.at[2], following),
                make(data.at[rows[3, 0]], slots.at[3], previous),
                make(slots.at[0], slots.at[4], following),
                make(slots.at[1], slots.at[5], previous),
            ]

        def gather_copies(rows, own, following, previous):
            return [
                make(data.at[own], data.at[own], following),
                make(data.at[own], data.at[own], previous),
                make(data.at[rows[3, 0]], data.at[rows[3, 0]], following),
                make(data.at[rows[1, 1]], data.at[rows[1, 1]], previous),
            ]

        cut_p, cut_q = cut(0, p, one), cut(base, q, two)
        self.rows_p = {(t, w): cut_p(t, w) for t in range(RING) for w in range(2)}
        self.rows_q = {(t, w): cut_q(t, w) for t in range(RING) for w in range(2)}
        own_p = pl.ds(pl.multiple_of(base, 8), one)
        own_q = pl.ds(pl.multiple_of(low, 8), two)
        self.own_y = pl.ds(pl.multiple_of(low + y * three, 8), three)
        self.rest_y = pl.ds(pl.multiple_of(low + (1 - y) * three, 8), three)
        self.reduce_p = reduce_copies(self.rows_p, first, p_next, p_prev)
        self.reduce_q = reduce_copies(self.rows_q, second, q_next, q_prev)
        self.swap = make(data.at[self.rest_y], third.at[0], y_mate)
        self.share = make(data.at[self.own_y], third.at[1], y_mate)
        self.gather_q = gather_copies(self.rows_q, own_q, q_next, q_prev)
        self.gather_p = gather_copies(self.rows_p, own_p, p_next, p_prev)

    def begin(self, copies):
        for copy in copies[:4]:
            copy.start()

    def middle(self, copies, rows, slots):
        copies[0].wait_recv()
        slots[0] = slots[0] + self.data[rows[1, 0], :]
        copies[4].start()
        copies[1].wait_recv()
        slots[1] = slots[1] + self.data[rows[3, 1], :]
        copies[5].start()

    def end(self, copies, rows, slots, ring, free):
        copies[2].wait_recv()
        copies[3].wait_recv()
        copies[4].wait_recv()
        self.data[rows[0, 0], :] = self.data[rows[0, 0], :] + (slots[3] + slots[4])
        copies[5].wait_recv()
        self.data[rows[0, 1], :] = self.data[rows[0, 1], :] + (slots[2] + slots[5])
        for copy in copies:
            copy.wait_send()
        for other in ring:
            pl.semaphore_signal(free, inc=1, device_id={"grid": other}, device_id_type=MESH)

    def spread(self, copies, free):
        pl.semaphore_wait(free, 2)
        copies[0].start()
        copies[1].start()

    def forward(self, copies):
        copies[0].wait_recv()
        copies[2].start()
        copies[1].wait_recv()
        copies[3].start()

    def settle(self, copies):
        copies[2].wait_recv()
        copies[3].wait_recv()
        for copy in copies:
            copy.wait_send()

    def step(self, i):
        p, q = self.reduce_p, self.reduce_q
        if i == 0:
            self.begin(p)
        elif i == 1:
            self.middle(p, self.rows_p, self.first)
        elif i == 2:
            self.end(p, self.rows_p, self.first, self.p_ring, self.free.at[0])
            self.begin(q)
        elif i == 3:
            self.middle(q, self.rows_q, self.second)
        elif i == 4:
            self.end(q, self.rows_q, self.second, self.q_ring, self.free.at[1])
            self.swap.start()
        elif i == 5:
            self.swap.wait_recv()
            self.data[self.own_y, :] = self.data[self.own_y, :] + self.third[0]
            self.share.start()
        elif i == 6:
            self.share.wait_recv()
            self.swap.wait_send()
            self.share.wait_send()
            self.data[self.rest_y, :] = self.third[1]
            self.spread(self.gather_q, self.free.at[1])
        elif i == 7:
            self.forward(self.gather_q)
        elif i == 8:
            self.settle(self.gather_q)
            self.spread(self.gather_p, self.free.at[0])
        elif i == 9:
            self.forward(self.gather_p)
        elif i == 10:
            self.settle(self.gather_p)


class DirectReduce(RingReduce):
    steps = 7

    def __init__(self, data, first, second, third, send, recv, free, p, p_next, p_prev, q, q_next, q_prev, y, device):
        self.data, self.first, self.second, self.free = data, first, second, free
        self.p_ring = (p_next, p_prev)
        size = data.shape[0]
        one, three = size // 4, size // 32
        half = one // 2
        base = p * one
        count = iter(range(COPIES))

        def make(src, dst, other):
            i = next(count)
            return remote(src, dst, send.at[i], recv.at[i], "grid", other)

        def rows(turn, which):
            return pl.ds(pl.multiple_of(((p + turn) % RING) * one + which * half, 8), half)

        def member(turn, flip):
            return pl.ds(pl.multiple_of(base + (((q + turn) % RING) * 2 + (y + flip) % 2) * three, 8), three)

        self.rows_p = {(t, w): rows(t, w) for t in range(RING) for w in range(2)}
        self.own = member(0, 0)
        self.origin = [member(RING - turn, flip) for turn, flip in PEERS]
        own_p = pl.ds(pl.multiple_of(base, 8), one)
        others = [device((q + turn) % RING, (y + flip) % 2) for turn, flip in PEERS]
        r = self.rows_p
        self.reduce_p = [
            make(data.at[r[2, 0]], first.at[0], p_next),
            make(data.at[r[2, 1]], first.at[1], p_prev),
            make(data.at[r[1, 1]], first.at[2], p_next),
            make(data.at[r[3, 0]], first.at[3], p_prev),
            make(first.at[0], first.at[4], p_next),
            make(first.at[1], first.at[5], p_prev),
        ]
        self.scatter = [make(data.at[member(*peer)], second.at[i], others[i]) for i, peer in enumerate(PEERS)]
        self.share = [make(data.at[self.own], second.at[7 + i], others[i]) for i in range(7)]
        self.gather_p = [
            make(data.at[own_p], data.at[own_p], p_next),
            make(data.at[own_p], data.at[own_p], p_prev),
            make(data.at[r[3, 0]], data.at[r[3, 0]], p_next),
            make(data.at[r[1, 1]], data.at[r[1, 1]], p_prev),
        ]

    def step(self, i):
        p = self.reduce_p
        if i == 0:
            self.begin(p)
        elif i == 1:
            self.middle(p, self.rows_p, self.first)
        elif i == 2:
            self.end(p, self.rows_p, self.first, self.p_ring, self.free.at[0])
            for copy in self.scatter:
                copy.start()
        elif i == 3:
            total = self.data[self.own, :]
            for j, copy in enumerate(self.scatter):
                copy.wait_recv()
                total = total + self.second[j]
            self.data[self.own, :] = total
            for copy in self.share:
                copy.start()
        elif i == 4:
            for copy in self.scatter:
                copy.wait_send()
            for j, copy in enumerate(self.share):
                copy.wait_recv()
                self.data[self.origin[j], :] = self.second[7 + j]
            for copy in self.share:
                copy.wait_send()
            self.spread(self.gather_p, self.free.at[0])
        elif i == 5:
            self.forward(self.gather_p)
        elif i == 6:
            self.settle(self.gather_p)


def whole_kernel(cand_ref, orb_ref, panel_out, gram_out, mixing_out,
                 panel, merged, from_core, from_chip, tiles_a, tiles_b, main, mate_a, mate_b,
                 *rest):
    slots = [rest[3 * u : 3 * u + 3] for u in range(6)]
    work, block, inv, coupling, mixing, orbitals, panel_send, panel_recv, send, recv, free, local_sem = rest[18:]
    load = pltpu.make_async_copy(orb_ref, orbitals, local_sem.at[10])
    load.start()
    o = lax.axis_index("orb")
    g = lax.axis_index("grid")
    core = o % 2
    mate = o + 1 - 2 * core
    across = (o + 2) % 4
    x = g // 8
    y = (g // 4) % 2
    z = g % 4
    x_next = ((x + 1) % RING) * 8 + y * 4 + z
    x_prev = ((x + 3) % RING) * 8 + y * 4 + z
    z_next = x * 8 + y * 4 + (z + 1) % RING
    z_prev = x * 8 + y * 4 + (z + 3) % RING

    def at_z(q, flip):
        return x * 8 + flip * 4 + q

    def at_x(q, flip):
        return q * 8 + flip * 4 + z

    barrier = pltpu.get_barrier_semaphore()
    near = [mate, across]
    for other in near:
        pl.semaphore_signal(barrier, inc=1, device_id={"orb": other}, device_id_type=MESH)
    far = [at_z((z + turn) % RING, (y + flip) % 2) for turn, flip in PEERS]
    far += [at_x((x + turn) % RING, (y + flip) % 2) for turn, flip in PEERS if turn]
    for other in far:
        pl.semaphore_signal(barrier, inc=1, device_id={"grid": other}, device_id_type=MESH)
    pl.semaphore_wait(barrier, len(near) + len(far))

    data = [[tiles_a.at[0], tiles_a.at[1]], [tiles_b.at[0], tiles_b.at[1]]]
    data += [[main.at[i, 0], main.at[i, 1]] for i in range(4)]
    units = []
    for u in range(6):
        kind = DirectReduce if u < 2 else RingReduce
        first, second, third = slots[u]
        units.append([
            kind(data[u][0], first.at[0], second.at[0], third.at[0], send.at[u, 0], recv.at[u, 0],
                 free.at[u, 0], x, x_next, x_prev, z, z_next, z_prev, y, at_z),
            kind(data[u][1], first.at[1], second.at[1], third.at[1], send.at[u, 1], recv.at[u, 1],
                 free.at[u, 1], z, z_next, z_prev, x, x_next, x_prev, y, at_x),
        ])
    done = [0] * 6

    def advance(u):
        for half in units[u]:
            half.step(done[u])
        done[u] += 1

    quarter = B // 2

    def part(t, which, j):
        return pl.ds(pl.multiple_of(t * B + j * quarter + which * PIECE, PIECE), PIECE)

    def orb_copy(src, dst, other, i):
        return remote(src, dst, panel_send.at[i], panel_recv.at[i], "orb", other)

    pieces = [(t, j) for t in range(2) for j in range(PIECES)]
    mine = {tj: part(tj[0], core, tj[1]) for tj in pieces}
    theirs = {tj: part(tj[0], 1 - core, tj[1]) for tj in pieces}
    n = len(pieces)
    give = {tj: orb_copy(cand_ref.at[theirs[tj]], from_core.at[i], mate, i) for i, tj in enumerate(pieces)}
    cross = {tj: orb_copy(merged.at[i], from_chip.at[i], across, n + i) for i, tj in enumerate(pieces)}
    share = {tj: orb_copy(panel.at[mine[tj]], panel.at[mine[tj]], mate, 2 * n + i) for i, tj in enumerate(pieces)}
    for tj in pieces:
        give[tj].start()

    def merge(i):
        tj = pieces[i]
        give[tj].wait_recv()
        merged[i] = cand_ref[mine[tj], :] + from_core[i]
        cross[tj].start()

    def collect(i):
        tj = pieces[i]
        cross[tj].wait_recv()
        panel[mine[tj], :] = merged[i] + from_chip[i]
        share[tj].start()

    contract = (((1,), (1,)), ((), ()))

    def product(rows, columns):
        return lax.dot_general(rows, columns, contract, preferred_element_type=jnp.float32)

    def core_rows(t):
        return panel[pl.ds(pl.multiple_of(t * B + core * quarter, quarter), quarter), :]

    def main_gram(i):
        if i == 0:
            load.wait()
        for h in range(2):
            def column(n, carry, h=h):
                at = pl.multiple_of(n * 256, 256)
                main[i, h, :, pl.ds(at, 256)] = product(
                    panel[i * quarter : (i + 1) * quarter, :], orbitals[pl.ds(h * WIDE + at, 256), :])
                return carry

            lax.fori_loop(0, WIDE // 256, column, 0)

    def gram_a():
        for h in range(2):
            tiles_a[h] = product(core_rows(0), panel[h * quarter : (h + 1) * quarter, :])

    save_panel = pltpu.make_async_copy(panel, panel_out, local_sem.at[0])

    def gram_b():
        for h in range(2):
            columns = panel[B + h * quarter : B + (h + 1) * quarter, :]
            tiles_b[h, :quarter, :] = product(core_rows(0), columns)
            tiles_b[h, quarter:, :] = product(core_rows(1), columns)
        save_panel.start()

    share_a = [orb_copy(tiles_a.at[h], mate_a.at[h], mate, 3 * n + h) for h in range(2)]
    share_b = [orb_copy(tiles_b.at[h], mate_b.at[h], mate, 3 * n + 2 + h) for h in range(2)]
    scale = 1.0 / CELLS
    own_rows = pl.ds(pl.multiple_of(core * quarter, quarter), quarter)
    mate_rows = pl.ds(pl.multiple_of((1 - core) * quarter, quarter), quarter)

    def start_a():
        for copy in share_a:
            copy.start()

    def start_b():
        for copy in share_b:
            copy.start()

    def load_a():
        for h in range(2):
            columns = slice(h * quarter, (h + 1) * quarter)
            work[own_rows, columns] = tiles_a[h] * scale
            share_a[h].wait_recv()
            work[mate_rows, columns] = mate_a[h] * scale

    main_saves = [
        [
            pltpu.make_async_copy(
                main.at[i, h], gram_out.at[pl.ds(i * quarter, quarter), pl.ds(h * WIDE, WIDE)],
                local_sem.at[2 + 2 * i + h])
            for h in range(2)
        ]
        for i in range(4)
    ]

    def move(u, now):
        for half in units[u]:
            half.step(now)
        if u >= 2 and now == RingReduce.steps - 1:
            for save in main_saves[u - 2]:
                save.start()

    def action(name):
        kind, i = name[:-1], int(name[-1])
        if kind == "m" or kind == "d":
            u = 1 + i if kind == "m" else i - 1
            u = u + 1 if kind == "m" else u
            now = done[u]
            done[u] += 1
            return lambda: move(u, now)
        table = {
            "gw": merge, "co": collect, "rc": lambda j: share[pieces[j]].wait_recv(), "g": main_gram,
            "a": lambda j: gram_a(), "b": lambda j: gram_b(), "xs": lambda j: start_a(),
            "xw": lambda j: load_a(), "ys": lambda j: start_b(),
        }
        return lambda: table[kind](i)

    def perform(names):
        for name in names:
            action(name)()

    def factor(phase, hooks):
        column = lax.broadcasted_iota(jnp.int32, (BLK, B), 1)
        low = phase * B

        def step(k, carry):
            start = pl.multiple_of(k * BLK, BLK)
            here = pl.ds(start, BLK)
            block[...] = work[here, here]

            def hook(c):
                for i in range(B // BLK):
                    if (i, c) in hooks:
                        pl.when(k == i)(hooks[i, c])

            invert_block(block, inv, hook)
            t = inv[...]
            row = jnp.dot(t, work[here, :], precision=HI, preferred_element_type=jnp.float32)
            mixing[pl.ds(low + start, BLK), low : low + B] = jnp.where(column < start, row, 0.0)
            mixing[pl.ds(low + start, BLK), pl.ds(low + start, BLK)] = t
            work[here, :] = row
            work[here, here] = t

            def update(i, carry):
                rows = pl.ds(pl.multiple_of(i * BLK, BLK), BLK)
                u = work[here, rows]
                work[rows, here] = jnp.zeros((BLK, BLK), jnp.float32)
                work[rows, :] -= lax.dot_general(
                    u, work[here, :], (((0,), (0,)), ((), ())), precision=HI, preferred_element_type=jnp.float32)
                return carry

            return lax.fori_loop(k + 1, B // BLK, update, carry)

        lax.fori_loop(0, B // BLK, step, 0)

    def hooks_of(phase):
        hooks = {}
        for (at, k, c), names in BETWEEN.items():
            if at == phase:
                todo = [action(name) for name in names]
                hooks[k, c] = lambda todo=todo: [do() for do in todo] and None
        return hooks

    perform(BEFORE)
    factor(0, hooks_of(0))
    perform(MIDDLE)
    for h in range(2):
        columns = slice(h * quarter, (h + 1) * quarter)
        coupling[own_rows, columns] = tiles_b[h, :quarter, :] * scale
        work[own_rows, columns] = tiles_b[h, quarter:, :] * scale
        share_b[h].wait_recv()
        coupling[mate_rows, columns] = mate_b[h, :quarter, :] * scale
        work[mate_rows, columns] = mate_b[h, quarter:, :] * scale
    mixing[:B, B:] = jnp.zeros((B, B), jnp.float32)
    first = mixing[:B, :B]
    coupling[...] = jnp.dot(first, coupling[...], precision=HI, preferred_element_type=jnp.float32)
    turned = (((0,), (0,)), ((), ()))
    work[...] -= lax.dot_general(
        coupling[...], coupling[...], turned, precision=HI, preferred_element_type=jnp.float32)
    coupling[...] = lax.dot_general(
        coupling[...], mixing[:B, :B], turned, precision=HI, preferred_element_type=jnp.float32)
    factor(1, hooks_of(1))
    mixing[B:, :B] = -jnp.dot(mixing[B:, B:], coupling[...], precision=HI, preferred_element_type=jnp.float32)
    save_mixing = pltpu.make_async_copy(mixing, mixing_out, local_sem.at[1])
    save_mixing.start()
    saves = [save_panel, save_mixing]
    perform(AFTER)
    for i in range(4):
        assert done[2 + i] == RingReduce.steps
        saves += main_saves[i]
    for copy in [*give.values(), *cross.values(), *share.values(), *share_a, *share_b]:
        copy.wait_send()
    for save in saves:
        save.wait()


BEFORE = [
    "gw0", "gw1", "gw2", "gw3", "co0", "rc0", "g0", "m0", "co1", "m0", "rc1", "a0",
    "d1", "g1", "m1", "m0", "d1", "co2", "rc2", "g2", "m1", "m2", "m0", "d1",
    "co3", "m1", "rc3", "b0", "d2", "g3", "m2", "m3", "m0", "m1", "d1", "d2",
    "m0", "m2", "m3", "m0", "m1", "d1", "d2", "m2", "m1", "m3", "m0", "d1",
    "m2", "d2", "m1", "m3", "m0", "d1", "xs0", "xw0", "d2",
]
BETWEEN = {
    (0, 0, 10): ["m2", "m1"],
    (0, 0, 12): ["m3"],
    (0, 1, 8): ["d2", "m0"],
    (0, 2, 0): ["d2", "ys0", "m1", "m2"],
    (0, 2, 4): ["m3"],
    (0, 3, 0): ["m0"],
    (0, 3, 12): ["m3"],
    (0, 3, 14): ["m1"],
    (1, 0, 0): ["m3", "m1"],
    (1, 0, 2): ["m2"],
    (1, 1, 0): ["m3"],
    (1, 2, 0): ["m2"],
    (1, 2, 14): ["m3"],
    (1, 3, 6): ["m2"],
}
MIDDLE = [
    "m2",
]
AFTER = [
    "m3",
]

def whole(cand, orbitals):
    cells = orbitals.shape[1]
    f32 = jnp.float32
    bf16 = jnp.bfloat16
    any_space = pl.BlockSpec(memory_space=pl.ANY)
    n = 2 * PIECES
    slots = []
    for rows, columns in UNIT_SHAPES:
        slots += [
            pltpu.VMEM((2, 6, rows // 8, columns), f32),
            pltpu.VMEM((2, 14, rows // 32, columns), f32),
            pltpu.VMEM((2, 2, rows // 32, columns), f32),
        ]
    return pl.pallas_call(
        whole_kernel,
        out_shape=(
            jax.ShapeDtypeStruct((ROWS, cells), bf16),
            jax.ShapeDtypeStruct((ROWS, LOCAL), f32),
            jax.ShapeDtypeStruct((ROWS, ROWS), f32),
        ),
        in_specs=[pl.BlockSpec(memory_space=pltpu.VMEM), any_space],
        out_specs=(any_space,) * 3,
        scratch_shapes=[
            pltpu.VMEM((ROWS, cells), bf16),
            pltpu.VMEM((n, PIECE, cells), bf16),
            pltpu.VMEM((n, PIECE, cells), bf16),
            pltpu.VMEM((n, PIECE, cells), bf16),
            pltpu.VMEM((2, 256, 256), f32),
            pltpu.VMEM((2, 512, 256), f32),
            pltpu.VMEM((4, 2, B // 2, WIDE), f32),
            pltpu.VMEM((2, 256, 256), f32),
            pltpu.VMEM((2, 512, 256), f32),
            *slots,
            pltpu.VMEM((B, B), f32),
            pltpu.VMEM((BLK, BLK), f32),
            pltpu.VMEM((BLK, BLK), f32),
            pltpu.VMEM((B, B), f32),
            pltpu.VMEM((ROWS, ROWS), f32),
            pltpu.VMEM((LOCAL, cells), bf16),
            pltpu.SemaphoreType.DMA((3 * n + 4,)),
            pltpu.SemaphoreType.DMA((3 * n + 4,)),
            pltpu.SemaphoreType.DMA((6, 2, COPIES)),
            pltpu.SemaphoreType.DMA((6, 2, COPIES)),
            pltpu.SemaphoreType.REGULAR((6, 2, 2)),
            pltpu.SemaphoreType.DMA((11,)),
        ],
        compiler_params=pltpu.CompilerParams(
            collective_id=0, has_side_effects=True, vmem_limit_bytes=60 << 20),
    )(cand, orbitals)


def pick_kernel(order_ref, block_ref, out_ref):
    owner = order_ref[pl.program_id(0)] // BPD == lax.axis_index("orb")
    out_ref[...] = jnp.where(owner, block_ref[...], jnp.zeros_like(block_ref))


def pick(orbitals, block_order):
    cells = orbitals.shape[1]
    return pl.pallas_call(
        pick_kernel,
        out_shape=jax.ShapeDtypeStruct((ROWS, cells), orbitals.dtype),
        grid_spec=pltpu.PrefetchScalarGridSpec(
            num_scalar_prefetch=1,
            grid=(2,),
            in_specs=[pl.BlockSpec((B, cells), lambda i, order: (order[i] % BPD, 0))],
            out_specs=pl.BlockSpec((B, cells), lambda i, order: (i, 0)),
        ),
        compiler_params=pltpu.CompilerParams(vmem_limit_bytes=60 << 20),
    )(block_order, orbitals)


PARTS = 4


def finish_kernel(order_ref, mixing_ref, gram_ref, panel_ref, factor_ref, ortho_ref, left, right):
    n = pl.program_id(0)
    own = lax.axis_index("orb")
    quarter = ROWS // 4
    bf16 = jnp.bfloat16

    @pl.when(n == 0)
    def _():
        for k in range(4):
            value = mixing_ref[:, k * quarter : (k + 1) * quarter]
            high = value.astype(bf16)
            left[:, 3 * k * quarter : (3 * k + 1) * quarter] = high
            left[:, (3 * k + 1) * quarter : (3 * k + 2) * quarter] = high
            left[:, (3 * k + 2) * quarter : (3 * k + 3) * quarter] = (value - high.astype(jnp.float32)).astype(bf16)

    def dot(a, b):
        return jnp.dot(a, b, preferred_element_type=jnp.float32)

    for k in range(4):
        value = gram_ref[k * quarter : (k + 1) * quarter, :]
        high = value.astype(bf16)
        right[3 * k * quarter : (3 * k + 1) * quarter, :] = high
        right[(3 * k + 1) * quarter : (3 * k + 2) * quarter, :] = (value - high.astype(jnp.float32)).astype(bf16)
        right[(3 * k + 2) * quarter : (3 * k + 3) * quarter, :] = high
    keep = jnp.where(own * BPD + n == order_ref[0], 0.0, 1.0 / CELLS)
    for r in range(4):
        rows = slice(r * quarter, (r + 1) * quarter)
        depth = 3 * (r + 1) * quarter
        total = dot(left[rows, :depth], right[:depth, :])
        factor_ref[rows, :] = total * (jnp.float32(1.0 / CELLS) if r < 2 else keep)
    mine = pl.ds(pl.multiple_of(own * quarter, quarter), quarter)
    total = jnp.zeros(ortho_ref.shape, jnp.float32)
    for k in range(4):
        panel = panel_ref[k * quarter : (k + 1) * quarter, :]
        for part in (0, 2):
            total += dot(left[mine, (3 * k + part) * quarter : (3 * k + part + 1) * quarter], panel)
    ortho_ref[...] = total


def finish(block_order, mixing, gram, panel):
    cells = panel.shape[1]
    f32 = jnp.float32
    return pl.pallas_call(
        finish_kernel,
        out_shape=(jax.ShapeDtypeStruct((ROWS, LOCAL), f32), jax.ShapeDtypeStruct((ROWS // 4, cells), f32)),
        grid_spec=pltpu.PrefetchScalarGridSpec(
            num_scalar_prefetch=1,
            grid=(PARTS,),
            in_specs=[
                pl.BlockSpec((ROWS, ROWS), lambda n, order: (0, 0)),
                pl.BlockSpec((ROWS, LOCAL // PARTS), lambda n, order: (0, n)),
                pl.BlockSpec((ROWS, cells // PARTS), lambda n, order: (0, n)),
            ],
            out_specs=(
                pl.BlockSpec((ROWS, LOCAL // PARTS), lambda n, order: (0, n)),
                pl.BlockSpec((ROWS // 4, cells // PARTS), lambda n, order: (0, n)),
            ),
            scratch_shapes=[
                pltpu.VMEM((ROWS, 3 * ROWS), jnp.bfloat16),
                pltpu.VMEM((3 * ROWS, LOCAL // PARTS), jnp.bfloat16),
            ],
        ),
        compiler_params=pltpu.CompilerParams(vmem_limit_bytes=60 << 20),
    )(block_order, mixing, gram, panel)


def local(orbitals, block_order):
    panel, gram, mixing = whole(pick(orbitals, block_order), orbitals)
    return finish(block_order, mixing, gram, panel)


def solution(mesh):
    return jax.shard_map(
        local,
        mesh=mesh,
        in_specs=(P("orb", "grid"), P()),
        out_specs=(P(None, "orb"), P("orb", "grid")),
        check_vma=False,
    )
```
